512 devices in a mesh: row: 16 (over y_lo, x, core), col: 32 (over z, y_hi).
Axes of the slice: x: 4, y: 4 (y_hi: 2, y_lo: 2; y = y_hi * 2 + y_lo), z: 16, core: 2. Of those that a mesh axis runs over, the one named last changes fastest.
Arguments:
- tokens: bfloat16 [1024, 98304], P('row', 'col'), may hold values from -6 to 6
- labels: int32 [1024, 512], P('row', 'col'), may hold values from 0 to 2
- gain_one: float32 [192], replicated, may hold values from 0.1 to 1.9
- qkv_weight: bfloat16 [192, 576], replicated, may hold values from -0.4375 to 0.4375
- proj_weight: bfloat16 [192, 192], replicated, may hold values from -0.4375 to 0.4375
- position_table: float32 [6, 225], replicated, may hold values from -4 to 300
- gain_two: float32 [192], replicated, may hold values from 0.1 to 1.9
- up_weight: bfloat16 [192, 768], replicated, may hold values from -0.4375 to 0.4375
- down_weight: bfloat16 [768, 192], replicated, may hold values from -0.21875 to 0.21875
Outputs:
- block_out: bfloat16 [1024, 98304], P('row', 'col')
The draws below stay inside these ranges and needn't reach their ends.
All inputs are finite; a program needn't handle non-finite values.
Results may differ from the reference program's by a relative error of at most 0.006.
Values may be sent and summed in bfloat16 or wider, within the bound.
A program may use at most 64 MiB of HBM per device.

```python
import jax
import jax.numpy as jnp
import numpy as np
from jax import lax

C = 192
HEADS = 6
HID = 768
WIN = 8
HD = 32
SHIFT = 4
H = 1024
W = 512


def draw_position_table(key, part):
    key = jax.random.fold_in(key, 5)
    span = (2 * WIN - 1) * (2 * WIN - 1)
    return jnp.clip(jax.random.normal(key, (HEADS, span), jnp.float32), -4.0, 4.0)


def set_ends(drawn, rng, low, largest):
    longest = drawn.shape.index(max(drawn.shape))
    spots = []
    for shift in (0, 1):
        where = [jax.random.randint(jax.random.fold_in(rng, axis), (), 0, length) for axis, length in enumerate(drawn.shape)]
        where[longest] = (where[longest] + shift) % drawn.shape[longest]
        spots.append(tuple(where))
    return drawn.at[spots[0]].set(low).at[spots[1]].set(largest)


def block_scale(key, extent, shards, least, largest):
    factor_of, own = 1.0, jax.random.fold_in(key, 6)
    for position, blocks in shards:
        heights = jnp.exp(jax.random.uniform(jax.random.fold_in(own, position), (blocks,), jnp.float32, least / len(shards), largest / len(shards)))
        factor_of = factor_of * jnp.repeat(heights, extent[position] // blocks).reshape([-1 if axis == position else 1 for axis in range(len(extent))])
    return factor_of


def scatter_about(stream_key, dims, deviation, reach, split=(), kind=jnp.bfloat16):
    entries = deviation * jax.random.normal(stream_key, dims, jnp.float32)
    if split:
        entries = entries * block_scale(stream_key, dims, split, -0.22, 0.18)
    return jnp.clip(entries, -reach, reach).astype(kind)


def setup_inputs(seed: int = 0) -> dict:
    streams_of = jax.random.split(jax.random.key(seed), 10)
    tokens = scatter_about(streams_of[0], (H, W * C), 1.0, 6.0, ((0, 16), (1, 32)))
    labels = set_ends(jax.random.randint(streams_of[1], (H, W), 0, 3), jax.random.fold_in(streams_of[1], 1), 0, 2).astype(jnp.int32)
    gain_one = jnp.clip(1.0 + 0.18 * jax.random.normal(streams_of[2], (C,), jnp.float32), 0.1, 1.9)
    qkv_weight = scatter_about(streams_of[3], (C, 3 * C), C ** -0.5, 0.4375)
    proj_weight = scatter_about(streams_of[4], (C, C), C ** -0.5, 0.4375)
    position_table = draw_position_table(jax.random.fold_in(streams_of[9], 71), 0)
    gain_two = jnp.clip(1.0 + 0.18 * jax.random.normal(streams_of[6], (C,), jnp.float32), 0.1, 1.9)
    up_weight = scatter_about(streams_of[7], (C, HID), C ** -0.5, 0.4375)
    down_weight = scatter_about(streams_of[8], (HID, C), HID ** -0.5, 0.21875)
    return {"tokens": tokens, "labels": labels, "gain_one": gain_one, "qkv_weight": qkv_weight, "proj_weight": proj_weight, "position_table": position_table, "gain_two": gain_two, "up_weight": up_weight, "down_weight": down_weight}


def layer_norm(values, gain):
    values = values.astype(jnp.float32)
    mean = lax.optimization_barrier(jnp.mean(values, axis=-1, keepdims=True))
    centred = values - mean
    variance = lax.optimization_barrier(jnp.mean(centred * centred, axis=-1, keepdims=True))
    return centred * lax.rsqrt(variance + 1e-05) * gain

def offsets():
    side = np.arange(WIN)
    ys = np.repeat(side, WIN)
    xs = np.tile(side, WIN)
    return (ys[:, None] - ys[None, :] + WIN - 1) * (2 * WIN - 1) + (xs[:, None] - xs[None, :] + WIN - 1)

def to_windows(grid):
    nrows, ncols = (grid.shape[0], grid.shape[1])
    rest = grid.shape[2:]
    blocks = grid.reshape((nrows // WIN, WIN, ncols // WIN, WIN) + rest)
    blocks = jnp.swapaxes(blocks, 1, 2)
    return blocks.reshape((nrows // WIN * (ncols // WIN), WIN * WIN) + rest)

def from_windows(windows, nrows, ncols):
    rest = windows.shape[2:]
    blocks = windows.reshape((nrows // WIN, ncols // WIN, WIN, WIN) + rest)
    blocks = jnp.swapaxes(blocks, 1, 2)
    return blocks.reshape((nrows, ncols) + rest)

def attend(normed, group, pair_bias, qkv_weight, proj_weight):
    nrows, ncols = (normed.shape[0], normed.shape[1])
    flat = to_windows(normed).reshape(-1, C)
    count = flat.shape[0] // (WIN * WIN)
    qkv = jnp.dot(flat, qkv_weight, preferred_element_type=jnp.float32).astype(jnp.bfloat16)
    qkv = qkv.reshape(count, WIN * WIN, 3, HEADS, HD)
    query = qkv[:, :, 0].astype(jnp.float32)
    keys = qkv[:, :, 1].astype(jnp.float32)
    values = qkv[:, :, 2].astype(jnp.float32)
    scores = jnp.einsum('wqhd,wkhd->whqk', query, keys) * HD ** (-0.5) + pair_bias[None]
    ids = to_windows(group)
    allowed = ids[:, :, None] == ids[:, None, :]
    scores = jnp.where(allowed[:, None], scores, -jnp.inf)
    top = lax.optimization_barrier(jnp.max(scores, axis=-1, keepdims=True))
    powers = jnp.exp(scores - top)
    probs = (powers / lax.optimization_barrier(jnp.sum(powers, axis=-1, keepdims=True))).astype(jnp.bfloat16)
    attended = jnp.einsum('whqk,wkhd->wqhd', probs.astype(jnp.float32), values).astype(jnp.bfloat16)
    branch = jnp.dot(attended.reshape(-1, C), proj_weight, preferred_element_type=jnp.float32)
    return from_windows(branch.reshape(count, WIN * WIN, C), nrows, ncols)

def feed_forward(residual, gain_two, up_weight, down_weight):
    second = layer_norm(residual, gain_two).astype(jnp.bfloat16).reshape(-1, C)
    hidden = jax.nn.gelu(jnp.dot(second, up_weight, preferred_element_type=jnp.float32), approximate=False).astype(jnp.bfloat16)
    mixed = jnp.dot(hidden, down_weight, preferred_element_type=jnp.float32).reshape(residual.shape)
    return (residual + mixed).astype(jnp.bfloat16)

def reference(tokens, labels, gain_one, qkv_weight, proj_weight, position_table, gain_two, up_weight, down_weight):
    grid = tokens.reshape(H, W, C)
    rolled = jnp.roll(grid, (-SHIFT, -SHIFT), axis=(0, 1))
    pair_bias = position_table[:, offsets()]
    col_flag = (jnp.arange(W, dtype=jnp.int32) >= W - SHIFT).astype(jnp.int32)

    def band(index):
        start = index * WIN
        strip = lax.dynamic_slice_in_dim(rolled, start, WIN, 0)
        strip_labels = lax.dynamic_slice_in_dim(labels, start, WIN, 0)
        row_flag = (start + jnp.arange(WIN, dtype=jnp.int32) >= H - SHIFT).astype(jnp.int32)
        group = strip_labels * 4 + row_flag[:, None] * 2 + col_flag[None, :]
        normed = layer_norm(strip, gain_one).astype(jnp.bfloat16)
        branch = attend(normed, group, pair_bias, qkv_weight, proj_weight)
        residual = strip.astype(jnp.float32) + branch
        return feed_forward(residual, gain_two, up_weight, down_weight)
    bands = lax.map(band, jnp.arange(H // WIN, dtype=jnp.int32))
    result = jnp.roll(bands.reshape(H, W, C), (SHIFT, SHIFT), axis=(0, 1))
    return result.reshape(H, W * C)
```

```python
import functools

import jax
import jax.numpy as jnp
from jax import lax
from jax.experimental import pallas as pl
from jax.experimental.pallas import tpu as pltpu
from jax.sharding import PartitionSpec as P

C = 192
HEADS = 6
HID = 768
WIN = 8
HD = 32
SHIFT = 4
MESH = pl.DeviceIdType.MESH
F32 = jnp.float32
BF16 = jnp.bfloat16
LOG2E = 1.4426950408889634
FAR = -1e30
NT = (((1,), (1,)), ((), ()))


def layer_norm(values, gain):
    mean = jnp.sum(values, axis=-1, keepdims=True) * (1.0 / C)
    centred = values - mean
    variance = jnp.sum(centred * centred, axis=-1, keepdims=True) * (1.0 / C)
    return centred * lax.rsqrt(variance + 1e-05) * gain


def iota(shape, axis):
    return lax.broadcasted_iota(jnp.int32, shape, axis)


def kernel(
    nrow, ncol,
    tok, lab, gain_one, qkv, proj, table, gain_two, up, down,
    out,
    tok_v, lab_v, g1_v, qkv_v, proj_v, tab_v, g2_v, up_v, down_v,
    left, right, top, bot, lt, lb, rt, rb, llab, tlab, ltlab,
    ext, branch, wt, wk, gath, bias, bias_l, bias_r,
    in_sem, send_sem, recv_sem,
):
    row, col = lax.axis_index("row"), lax.axis_index("col")

    def at(dr, dc):
        return (lax.rem(row + dr + nrow, nrow), lax.rem(col + dc + ncol, ncol))

    around = [(0, 1), (1, 1), (-1, 1), (0, -1), (1, -1), (-1, -1), (1, 0), (-1, 0)]
    barrier = pltpu.get_barrier_semaphore()
    for dr, dc in around:
        pl.semaphore_signal(barrier, inc=1, device_id=at(dr, dc), device_id_type=MESH)
    loads = [
        pltpu.make_async_copy(src, dst, in_sem.at[i])
        for i, (src, dst) in enumerate([
            (tok, tok_v), (lab, lab_v), (gain_one, g1_v), (qkv, qkv_v), (proj, proj_v),
            (table, tab_v), (gain_two, g2_v), (up, up_v), (down, down_v),
        ])
    ]
    for load in loads:
        load.start()
    pl.semaphore_wait(barrier, len(around))

    first, last = pl.ds(0, 16), pl.ds(48, 16)
    west, east = pl.ds(0, 4 * C), pl.ds(12 * C, 4 * C)
    whole = pl.ds(0, 64)
    moves = [
        (tok.at[whole, east], left, (0, 1)),
        (tok.at[last, east], lt, (1, 1)),
        (tok.at[first, east], lb, (-1, 1)),
        (lab, llab, (0, 1)),
        (lab.at[pl.ds(56, 8)], ltlab, (1, 1)),
        (tok.at[whole, west], right, (0, -1)),
        (tok.at[last, west], rt, (1, -1)),
        (tok.at[first, west], rb, (-1, -1)),
        (tok.at[last], top, (1, 0)),
        (tok.at[first], bot, (-1, 0)),
        (lab.at[pl.ds(56, 8)], tlab, (1, 0)),
    ]
    copies = [
        pltpu.make_async_remote_copy(
            src_ref=src, dst_ref=dst, send_sem=send_sem.at[i], recv_sem=recv_sem.at[i],
            device_id=at(*where), device_id_type=MESH,
        )
        for i, (src, dst, where) in enumerate(moves)
    ]
    for copy in copies:
        copy.start()
    for load in loads:
        load.wait()

    eye = (iota((16, 64), 0) == iota((16, 64), 1)).astype(F32)
    apart = jnp.where(iota((64, 64), 0) < 16, (iota((64, 64), 0) != iota((64, 64), 1)).astype(F32) * FAR, 0.0)
    weights = qkv_v[...].astype(F32)
    pad = jnp.zeros((C, 64), F32)
    wt[0:C] = jnp.concatenate([weights[:, 0:C].T, pad], axis=1).astype(BF16)
    wt[C : C + 16] = jnp.concatenate([jnp.zeros((16, C), F32), eye], axis=1).astype(BF16)
    wt[C + 16 : 2 * C + 16] = jnp.concatenate([weights[:, 2 * C : 3 * C].T, pad], axis=1).astype(BF16)
    wk[0:C] = jnp.concatenate([weights[:, C : 2 * C], pad], axis=1).astype(BF16)
    wk[C : C + 64] = jnp.concatenate([jnp.zeros((64, C), F32), apart], axis=1).astype(BF16)

    spread = jnp.concatenate([tab_v[...] * LOG2E, jnp.zeros((HEADS, 256 - 225), F32)], axis=1)
    spread = jnp.concatenate([spread, jnp.zeros((8 - HEADS, 256), F32)], axis=0)
    rows = jnp.concatenate([spread] + [pltpu.roll(spread, 15 * y, 1) for y in range(1, WIN)], axis=0)
    lane = iota((256, 128), 1)
    select = (iota((256, 128), 0) == (lane % 8 + 7) * 15 + lane // 8).astype(F32)
    gath[...] = jnp.dot(rows, select, precision=lax.Precision.HIGHEST).reshape(8, 8, 128)
    for h in range(HEADS):
        strip = gath[:, h, :]
        for x in range(WIN):
            part = strip[:, (7 - x) * 8 : (7 - x) * 8 + 64]
            bias[x * 8 : x * 8 + 8, h * 64 : h * 64 + 64] = part
            bias_r[x * 8 : x * 8 + 8, h * 32 : h * 32 + 32] = part[:, 0:32]
            bias_l[x * 8 : x * 8 + 8, h * 32 : h * 32 + 32] = part[:, 32:64]

    gain = g1_v[...].reshape(1, C)
    gain_b = g2_v[...].reshape(1, C)

    def rim(above, below):
        above, below = above[...].astype(F32)[8:16], below[...].astype(F32)[0:8]
        return jnp.where(iota(above.shape, 0) >= 4, above, below)

    def place_rows(values, base, count):
        for j in range(count):
            ext[base + j, 4:68] = layer_norm(values[:, j * C : j * C + C], gain)

    def place_rim(values, base, count):
        for j in range(count):
            edge = layer_norm(values[:, j * C : j * C + C], gain)
            ext[base + j, 0:4] = edge[4:8]
            ext[base + j, 68:72] = edge[0:4]

    for j in range(0, 16, 2):
        place_rows(tok_v[:, j * C : j * C + 2 * C].astype(F32), j + 4, 2)

    def attend(b, x0, nx, table_ref, label_rows, lane0):
        nq = nx * 8
        edge_row = iota((72, 1), 0)
        at_end = ((edge_row < 8) & (row == 0)) | ((edge_row >= 64) & (row == nrow - 1))
        row_flag = ((edge_row % 8 >= 4) & at_end).astype(jnp.int32) * 2
        at_side = {0: col == 0, 1: None, 2: col == ncol - 1}[b]
        blocks = []
        for x in range(WIN):
            group = label_rows[:, lane0 + x : lane0 + x + 1] * 4 + row_flag
            if x >= 4 and at_side is not None:
                group = group + at_side.astype(jnp.int32)
            onehot = (iota((72, 64), 1) == group).astype(F32)
            block = jnp.concatenate([ext[8 * b + x], onehot], axis=1)
            blocks.append(block.reshape(9, 1, 8, 256))
        tokens = jnp.concatenate(blocks, axis=1).reshape(9 * 64, 256).astype(BF16)
        keys = jnp.dot(tokens, wk[...], preferred_element_type=F32).astype(BF16)
        both = lax.dot_general(wt[...], tokens, NT, preferred_element_type=F32)
        values = both[C + 16 :].astype(BF16)
        head_of_row = iota((C, HEADS * nq), 0) // HD
        own = head_of_row == iota((C, HEADS * nq), 1) // nq
        parts = []
        for a in range(9):
            q = both[0 : C + 16, a * 64 + x0 * 8 : a * 64 + x0 * 8 + nq]
            q = jnp.concatenate([q] * HEADS, axis=1)
            q = jnp.concatenate([jnp.where(own, q[0:C], 0.0), q[C:], jnp.zeros((48, HEADS * nq), F32)], axis=0)
            scores = jnp.dot(keys[a * 64 : a * 64 + 64], q.astype(BF16), preferred_element_type=F32)
            scores = scores * (HD ** (-0.5) * LOG2E) + table_ref[...]
            powers = jnp.exp2(scores - jnp.max(scores, axis=0, keepdims=True))
            total = jnp.sum(powers, axis=0, keepdims=True)
            probs = (powers * (1.0 / total)).astype(BF16)
            full = jnp.dot(values[:, a * 64 : a * 64 + 64], probs, preferred_element_type=F32)
            parts.append(jnp.concatenate(
                [full[h * HD : h * HD + HD, h * nq : h * nq + nq] for h in range(HEADS)], axis=0
            ))
        attended = jnp.concatenate(parts, axis=1).T.astype(BF16)
        mixed = jnp.dot(attended, proj_v[...], preferred_element_type=F32).reshape(9, nx, 8, C)
        for x in range(nx):
            branch[8 * b + x0 + x] = mixed[:, x].reshape(72, C)

    def finish(f):
        piece = tok_v[:, f * 768 : f * 768 + 768].astype(F32)
        residual = jnp.concatenate(
            [piece[:, j * C : j * C + C] + branch[4 * f + j + 4, 4:68] for j in range(4)], axis=0
        )
        second = layer_norm(residual, gain_b).astype(BF16)
        hidden = jnp.dot(second, up_v[...], preferred_element_type=F32)
        hidden = (hidden * (0.5 + 0.5 * lax.erf(hidden * 0.7071067811865476))).astype(BF16)
        done = residual + jnp.dot(hidden, down_v[...], preferred_element_type=F32)
        out[:, f * 768 : f * 768 + 768] = jnp.concatenate(
            [done[j * 64 : j * 64 + 64] for j in range(4)], axis=1
        ).astype(BF16)

    for i in (8, 9, 10):
        copies[i].wait_recv()
    place_rim(rim(top, bot), 4, 16)
    label_rows = jnp.concatenate([tlab[...], lab_v[...]], axis=0)
    attend(1, 0, 8, bias, label_rows, 0)
    finish(1)
    finish(2)
    for i in (5, 6, 7):
        copies[i].wait_recv()
    place_rows(right[...].astype(F32), 20, 4)
    place_rim(rim(rt, rb), 20, 4)
    attend(2, 0, 4, bias_r, label_rows, 8)
    finish(3)
    for i in range(5):
        copies[i].wait_recv()
    place_rows(left[...].astype(F32), 0, 4)
    place_rim(rim(lt, lb), 0, 4)
    attend(0, 4, 4, bias_l, jnp.concatenate([ltlab[...], llab[...]], axis=0), 8)
    finish(0)
    for copy in copies:
        copy.wait_send()


def local(nrow, ncol, *args):
    vmem = pltpu.VMEM
    scratch = [vmem(a.shape, a.dtype) for a in args]
    scratch += [vmem((64, 768), BF16)] * 2 + [vmem((16, 3072), BF16)] * 2 + [vmem((16, 768), BF16)] * 4
    scratch += [vmem((64, 16), jnp.int32), vmem((8, 16), jnp.int32), vmem((8, 16), jnp.int32)]
    scratch += [vmem((24, 72, C), F32)] * 2
    scratch += [vmem((2 * C + 16, 256), BF16), vmem((256, 256), BF16)]
    scratch += [vmem((8, 8, 128), F32), vmem((64, 384), F32), vmem((64, 192), F32), vmem((64, 192), F32)]
    scratch += [pltpu.SemaphoreType.DMA((9,)), pltpu.SemaphoreType.DMA((11,)), pltpu.SemaphoreType.DMA((11,))]
    return pl.pallas_call(
        functools.partial(kernel, nrow, ncol),
        out_shape=jax.ShapeDtypeStruct((64, 3072), BF16),
        in_specs=[pl.BlockSpec(memory_space=pl.ANY)] * len(args),
        out_specs=pl.BlockSpec(memory_space=vmem),
        scratch_shapes=scratch,
        compiler_params=pltpu.CompilerParams(
            collective_id=0, has_side_effects=True, vmem_limit_bytes=48 * 1024 * 1024
        ),
        name="window_block",
    )(*args)


def solution(mesh):
    placed = (P("row", "col"), P("row", "col"), P(), P(), P(), P(), P(), P(), P())
    return jax.shard_map(
        functools.partial(local, mesh.shape["row"], mesh.shape["col"]),
        mesh=mesh, in_specs=placed, out_specs=P("row", "col"), check_vma=False,
    )
```

```python
import functools

import jax
import jax.numpy as jnp
from jax import lax
from jax.experimental import pallas as pl
from jax.experimental.pallas import tpu as pltpu
from jax.sharding import PartitionSpec as P

C = 192
HEADS = 6
HID = 768
WIN = 8
HD = 32
MESH = pl.DeviceIdType.MESH
F32 = jnp.float32
BF16 = jnp.bfloat16
LOG2E = 1.4426950408889634
FAR = -1e30
NT = (((1,), (1,)), ((), ()))
LOGIT = (
    -2.3022072315216064, -0.10483857989311218, 9.559292084304616e-05, 0.00015938941214699298,
    -1.1452430044300854e-05, 3.8504501276293013e-07, -5.209909392789314e-09,
)


def iota(shape, axis):
    return lax.broadcasted_iota(jnp.int32, shape, axis)


def dot(a, b):
    return jnp.dot(a, b, preferred_element_type=F32)


def kernel(
    nrow, ncol,
    tok, lab, gain_one, qkv, proj, table, gain_two, up, down,
    out,
    tok_v, lab_v, g1_v, qkv_v, proj_v, tab_v, g2_v, up_v, down_v,
    left, right, top, bot, lt, lb, rt, rb, llab, tlab, ltlab,
    ext, branch, wq, wv, wk, ones, gath, bias, bias_l, bias_r, blocks64, blocks32, scores_v,
    in_sem, send_sem, recv_sem, met_sem,
):
    row, col = lax.axis_index("row"), lax.axis_index("col")
    newest, oldest = col == ncol - 1, col == 0

    def at(dr, dc):
        return (lax.rem(row + dr + nrow, nrow), lax.rem(col + dc + ncol, ncol))

    barrier = pltpu.get_barrier_semaphore()

    def greet(dr, dc):
        pl.semaphore_signal(barrier, inc=1, device_id=at(dr, dc), device_id_type=MESH)

    for dr in (0, 1, -1):
        greet(dr, -1)
        pl.when(jnp.logical_not(newest | (col == ncol - 2)))(functools.partial(greet, dr, 1))
        if dr:
            pl.when(jnp.logical_not(newest))(functools.partial(greet, dr, 0))
    loads = [
        pltpu.make_async_copy(src, dst, in_sem.at[i])
        for i, (src, dst) in enumerate([
            (tok, tok_v), (lab, lab_v), (gain_one, g1_v), (qkv, qkv_v), (proj, proj_v),
            (table, tab_v), (gain_two, g2_v), (up, up_v), (down, down_v),
        ])
    ]
    for load in loads:
        load.start()
    pl.semaphore_wait(barrier, jnp.where(newest, 3, jnp.where(oldest, 5, 8)))

    first, last, whole = pl.ds(0, 16), pl.ds(48, 16), pl.ds(0, 64)
    west, east = pl.ds(0, 4 * C), pl.ds(12 * C, 4 * C)
    moves = [
        (tok.at[whole, east], left, (0, 1)),
        (tok.at[last, east], lt, (1, 1)),
        (tok.at[first, east], lb, (-1, 1)),
        (lab, llab, (0, 1)),
        (lab, ltlab, (1, 1)),
        (tok.at[last], top, (1, 0)),
        (tok.at[first], bot, (-1, 0)),
        (lab, tlab, (1, 0)),
        (tok.at[whole, west], right, (0, -1)),
        (tok.at[last, west], rt, (1, -1)),
        (tok.at[first, west], rb, (-1, -1)),
    ]
    copies = [
        pltpu.make_async_remote_copy(
            src_ref=src, dst_ref=dst, send_sem=send_sem.at[i], recv_sem=recv_sem.at[i],
            device_id=at(*where), device_id_type=MESH,
        )
        for i, (src, dst, where) in enumerate(moves)
    ]
    EAST, ROWS, WEST = range(0, 5), range(5, 8), range(8, 11)

    def send(group):
        for i in group:
            copies[i].start()

    def arrive(group):
        for i in group:
            copies[i].wait_recv()

    def meet():
        pl.semaphore_signal(met_sem, inc=1, device_id=at(0, 1), device_id_type=MESH)

    send(EAST)
    pl.when(jnp.logical_not(newest))(functools.partial(send, ROWS))
    pl.when(jnp.logical_not(newest | oldest))(functools.partial(send, WEST))
    pl.when(col == ncol - 2)(meet)
    for load in loads:
        load.wait()

    eye = (iota((16, 64), 0) == iota((16, 64), 1)).astype(F32)
    apart = jnp.where(iota((64, 64), 0) < 16, (iota((64, 64), 0) != iota((64, 64), 1)).astype(F32) * FAR, 0.0)
    weights = qkv_v[...].astype(F32)
    pad = jnp.zeros((C, 64), F32)
    wq[0:C] = jnp.concatenate([weights[:, 0:C].T, pad], axis=1).astype(BF16)
    wq[C : C + 16] = jnp.concatenate([jnp.zeros((16, C), F32), eye], axis=1).astype(BF16)
    wv[...] = jnp.concatenate([weights[:, 2 * C : 3 * C].T, pad], axis=1).astype(BF16)
    wk[0:C] = jnp.concatenate([weights[:, C : 2 * C], pad], axis=1).astype(BF16)
    wk[C : C + 64] = jnp.concatenate([jnp.zeros((64, C), F32), apart], axis=1).astype(BF16)
    ones[...] = (iota((2 * C, 2 * C), 0) // C == iota((2 * C, 2 * C), 1) // C).astype(F32).astype(BF16)
    blocks64[...] = jnp.zeros(blocks64.shape, BF16)
    blocks32[...] = jnp.zeros(blocks32.shape, BF16)

    spread = jnp.concatenate([tab_v[...] * LOG2E, jnp.zeros((HEADS, 256 - 225), F32)], axis=1)
    spread = jnp.concatenate([spread, jnp.zeros((8 - HEADS, 256), F32)], axis=0)
    rows = jnp.concatenate([pltpu.roll(spread, 15 * ((s + 4) % 8), 1) if s != 4 else spread for s in range(WIN)], axis=0)
    lane = iota((256, 128), 1)
    select = (iota((256, 128), 0) == ((lane % 8 + 4) % 8 + 7) * 15 + lane // 8).astype(F32)
    gath[...] = jnp.dot(rows, select, precision=lax.Precision.HIGHEST).reshape(8, 8, 128)
    bias_l[...] = jnp.zeros(bias_l.shape, F32)
    bias_r[...] = jnp.zeros(bias_r.shape, F32)
    for h in range(HEADS):
        strip = gath[:, h, :]
        for x in range(WIN):
            part = strip[:, (7 - x) * 8 : (7 - x) * 8 + 64]
            bias[x * 8 : x * 8 + 8, h * 64 : h * 64 + 64] = part
            bias_r[x * 8 : x * 8 + 8, h * 32 : h * 32 + 32] = part[:, 0:32]
            bias_l[x * 8 : x * 8 + 8, h * 32 : h * 32 + 32] = part[:, 32:64]

    gain = jnp.concatenate([g1_v[...].reshape(1, C)] * 2, axis=1)
    gain_b = g2_v[...].reshape(1, C)

    def place(pieces, spots):
        tokens = jnp.concatenate(pieces, axis=0) if len(pieces) > 1 else pieces[0]
        wide = tokens.astype(F32)
        centred = wide - dot(tokens, ones[...]) * (1.0 / C)
        variance = dot((centred * centred).astype(BF16), ones[...]) * (1.0 / C)
        normed = centred * lax.rsqrt(variance + 1e-05) * gain
        size = pieces[0].shape[0]
        for i, (column, start) in enumerate(spots):
            part = normed[i * size : i * size + size]
            ext[column, start : start + size, 0:C] = part[:, 0:C]
            ext[column + 1, start : start + size, 0:C] = part[:, C:]

    def rim(above, below, base, count):
        above, below = above[...].astype(F32)[8:16], below[...].astype(F32)[0:8]
        block = jnp.where(iota(above.shape, 0) >= 4, above, below).astype(F32)
        pairs = range(count // 2)
        pieces = jnp.concatenate([block[:, 2 * C * i : 2 * C * i + 2 * C] for i in pairs], axis=0).astype(BF16)
        wide = pieces.astype(F32)
        centred = wide - dot(pieces, ones[...]) * (1.0 / C)
        variance = dot((centred * centred).astype(BF16), ones[...]) * (1.0 / C)
        normed = centred * lax.rsqrt(variance + 1e-05) * gain
        for i in pairs:
            part = normed[8 * i : 8 * i + 8]
            ext[base + 2 * i, 64:72, 0:C] = part[:, 0:C]
            ext[base + 2 * i + 1, 64:72, 0:C] = part[:, C:]

    def labels_of(above, own):
        above, own = above[...].astype(F32).T, own[...].astype(F32).T
        rows = jnp.concatenate([above[56:64], own], axis=0)
        rows = pltpu.roll(rows.reshape(9, 8, 16), 4, 1).reshape(72, 16)
        spot = iota((72, 1), 0)
        at_end = ((spot < 8) & (row == 0)) | ((spot >= 64) & (row == nrow - 1))
        return rows * 4.0 + jnp.where((spot % 8 < 4) & at_end, 2.0, 0.0)

    def attend(b, spans, x0, nx, table_ref, groups, lane0, blocks):
        nq = nx * 8
        per = 128 // nq
        wide = -(-HEADS // per)
        heads = [list(range(m * per, min(HEADS, m * per + per))) for m in range(wide)]
        count = len(spans)
        at_side = {0: oldest, 1: None, 2: newest}[b]
        lanes = iota((72, 256), 1)
        cut = []
        for x in range(WIN):
            value = ext[8 * b + x]
            turned = jnp.concatenate([value[64:72], value[0:64]], axis=0)
            value = jnp.where(iota((72, 256), 0) % 8 < 4, value, turned)
            group = groups[:, lane0 + x : lane0 + x + 1]
            if x >= 4 and at_side is not None:
                group = group + jnp.where(at_side, 1.0, 0.0)
            mark = ((lanes - C) == group.astype(jnp.int32)).astype(F32)
            cut.append(jnp.where(lanes >= C, mark, value))
        tokens = jnp.concatenate(
            [cut[x][8 * a : 8 * a + 8] for a in spans for x in range(WIN)], axis=0
        ).astype(BF16)
        asking = jnp.concatenate(
            [cut[x][8 * a : 8 * a + 8] for a in spans for x in range(x0, x0 + nx)], axis=0
        ).astype(BF16) if nx < WIN else tokens
        keys = dot(tokens, wk[...]).astype(BF16)
        queries = lax.dot_general(wq[...], asking, NT, preferred_element_type=F32)
        values = lax.dot_general(wv[...], tokens, NT, preferred_element_type=F32)

        block = iota((16, 128), 1) // nq
        block32 = iota((HD, 128), 1) // nq
        for g in range(count // per):
            some = queries[:, 128 * g : 128 * g + 128]
            turns = [some] + [pltpu.roll(some, k * nq, 1) for k in range(1, per)]
            for s in range(per):
                w = per * g + s
                code = turns[(0 - s) % per][C:]
                for t in range(1, per):
                    code = jnp.where(block == t, turns[(t - s) % per][C:], code)
                code = code.astype(BF16)
                for m in range(wide):
                    part = [
                        jnp.where(block32 == h % per, turns[(h - s) % per][h * HD : h * HD + HD], 0.0)
                        for h in heads[m]
                    ]
                    low = heads[m][0] * HD
                    blocks[w, low : low + HD * len(part), 128 * m : 128 * m + 128] = jnp.concatenate(
                        part, axis=0
                    ).astype(BF16)
                    blocks[w, C : C + 16, 128 * m : 128 * m + 128] = code
        for w in range(count):
            scores = dot(keys[w * 64 : w * 64 + 64], blocks[w])
            scores_v[w, :, 0 : 128 * wide] = scores * (HD ** (-0.5) * LOG2E) + table_ref[...]
        powers = []
        for w in range(count):
            scores = scores_v[w, :, 0 : 128 * wide]
            powers.append(jnp.exp2(scores - jnp.max(scores, axis=0, keepdims=True)).astype(BF16))
        one = jnp.ones((16, 64), BF16)
        found = []
        for w in range(count):
            mine = values[:, w * 64 : w * 64 + 64].astype(BF16)
            for m in range(wide):
                low, high = heads[m][0] * HD, heads[m][-1] * HD + HD
                sums = dot(jnp.concatenate([mine[low:high], one], axis=0), powers[w][:, 128 * m : 128 * m + 128])
                found.append(sums[0 : high - low] * (1.0 / sums[high - low : high - low + 1]))
        turned = []
        for g in range(count // per):
            rows_of = []
            for h in range(HEADS):
                m, i = h // per, h % per
                row_block = None
                for s in range(per):
                    piece = found[(per * g + s) * wide + m][i * HD : i * HD + HD]
                    if (s - h) % per:
                        piece = pltpu.roll(piece, ((s - h) % per) * nq, 1)
                    row_block = piece if s == 0 else jnp.where(block32 == s, piece, row_block)
                rows_of.append(row_block)
            turned.append(jnp.concatenate(rows_of, axis=0))
        attended = jnp.concatenate(turned, axis=1).T.astype(BF16)
        mixed = dot(attended, proj_v[...])
        for w, a in enumerate(spans):
            if a in spans[:w]:
                continue
            for x in range(nx):
                spot = w * nq + x * 8
                branch[8 * b + x0 + x - 4, 8 * a : 8 * a + 8] = mixed[spot : spot + 8]

    def finish(f):
        piece = tok_v[:, f * 768 : f * 768 + 768].astype(F32)
        upper = iota((64, C), 0) % 8 < 4
        residual = jnp.concatenate(
            [
                piece[:, j * C : j * C + C]
                + jnp.where(upper, branch[4 * f + j, 0:64], branch[4 * f + j, 8:72])
                for j in range(4)
            ],
            axis=0,
        )
        unit = ones[0:C, 0:C]
        high = residual.astype(BF16)
        low = (residual - high.astype(F32)).astype(BF16)
        centred = residual - (dot(high, unit) + dot(low, unit)) * (1.0 / C)
        variance = dot((centred * centred).astype(BF16), unit) * (1.0 / C)
        second = (centred * lax.rsqrt(variance + 1e-05) * gain_b).astype(BF16)
        hidden = dot(second, up_v[...])
        square = hidden * hidden
        logit = LOGIT[6] * square + LOGIT[5]
        for k in range(4, -1, -1):
            logit = logit * square + LOGIT[k]
        hidden = (hidden * (1.0 / (1.0 + jnp.exp2(hidden * logit)))).astype(BF16)
        done = residual + lax.dot_general(hidden, down_v[...], NT, preferred_element_type=F32)
        out[:, f * 768 : f * 768 + 768] = jnp.concatenate(
            [done[j * 64 : j * 64 + 64] for j in range(4)], axis=1
        ).astype(BF16)

    place([tok_v[:, 2 * C * i : 2 * C * i + 2 * C] for i in range(8)], [(4 + 2 * i, 0) for i in range(8)])

    @pl.when(newest)
    def _():
        pl.semaphore_wait(met_sem, 1)
        send(ROWS)
        send(WEST)

    arrive(ROWS)
    groups = labels_of(tlab, lab_v)
    rim(top, bot, 4, 16)
    attend(1, list(range(9)) + [8], 0, 8, bias, groups, 0, blocks64)
    finish(1)
    finish(2)

    @pl.when(jnp.logical_not(oldest))
    def _():
        arrive(WEST)
        place([right[:, 2 * C * i : 2 * C * i + 2 * C] for i in range(2)], [(20 + 2 * i, 0) for i in range(2)])
        rim(rt, rb, 20, 4)

    arrive(EAST)

    @pl.when(oldest)
    def _():
        send(WEST)
        arrive(WEST)
        place([right[:, 2 * C * i : 2 * C * i + 2 * C] for i in range(2)], [(20 + 2 * i, 0) for i in range(2)])
        rim(rt, rb, 20, 4)

    attend(2, list(range(9)) + [8] * 3, 0, 4, bias_r, groups, 8, blocks32)
    finish(3)
    place([left[:, 2 * C * i : 2 * C * i + 2 * C] for i in range(2)], [(2 * i, 0) for i in range(2)])
    rim(lt, lb, 0, 4)
    attend(0, list(range(9)) + [8] * 3, 4, 4, bias_l, labels_of(ltlab, llab), 8, blocks32)
    finish(0)
    for copy in copies:
        copy.wait_send()


def local(nrow, ncol, tok, lab, gain_one, qkv, proj, table, gain_two, up, down):
    args = (tok, lab.T, gain_one, qkv, proj, table, gain_two, up, down.T)
    vmem = pltpu.VMEM
    scratch = [vmem(a.shape, a.dtype) for a in args]
    scratch += [vmem((64, 768), BF16)] * 2 + [vmem((16, 3072), BF16)] * 2 + [vmem((16, 768), BF16)] * 4
    scratch += [vmem((16, 64), jnp.int32)] * 3
    scratch += [vmem((24, 72, 256), F32), vmem((16, 72, C), F32)]
    scratch += [vmem((C + 16, 256), BF16), vmem((C, 256), BF16), vmem((256, 256), BF16), vmem((2 * C, 2 * C), BF16)]
    scratch += [vmem((8, 8, 128), F32), vmem((64, 384), F32), vmem((64, 256), F32), vmem((64, 256), F32)]
    scratch += [vmem((10, 256, 384), BF16), vmem((12, 256, 256), BF16), vmem((12, 64, 384), F32)]
    scratch += [pltpu.SemaphoreType.DMA((9,)), pltpu.SemaphoreType.DMA((11,)), pltpu.SemaphoreType.DMA((11,))]
    scratch += [pltpu.SemaphoreType.REGULAR]
    return pl.pallas_call(
        functools.partial(kernel, nrow, ncol),
        out_shape=jax.ShapeDtypeStruct((64, 3072), BF16),
        in_specs=[pl.BlockSpec(memory_space=pltpu.HBM)] * len(args),
        out_specs=pl.BlockSpec(memory_space=vmem),
        scratch_shapes=scratch,
        compiler_params=pltpu.CompilerParams(
            collective_id=0, has_side_effects=True, vmem_limit_bytes=64 * 1024 * 1024
        ),
        name="window_block",
    )(*args)


def solution(mesh):
    placed = (P("row", "col"), P("row", "col"), P(), P(), P(), P(), P(), P(), P())
    return jax.shard_map(
        functools.partial(local, mesh.shape["row"], mesh.shape["col"]),
        mesh=mesh, in_specs=placed, out_specs=P("row", "col"), check_vma=False,
    )
```

```python
import functools

import jax
import jax.numpy as jnp
from jax import lax
from jax.experimental import pallas as pl
from jax.experimental.pallas import tpu as pltpu
from jax.sharding import PartitionSpec as P

C = 192
HEADS = 6
HID = 768
WIN = 8
HD = 32
MESH = pl.DeviceIdType.MESH
F32 = jnp.float32
BF16 = jnp.bfloat16
LOG2E = 1.4426950408889634
FAR = -1e30
NT = (((1,), (1,)), ((), ()))
LOGIT = (
    -2.3022072315216064, -0.10483857989311218, 9.559292084304616e-05, 0.00015938941214699298,
    -1.1452430044300854e-05, 3.8504501276293013e-07, -5.209909392789314e-09,
)


def iota(shape, axis):
    return lax.broadcasted_iota(jnp.int32, shape, axis)


def dot(a, b):
    return jnp.dot(a, b, preferred_element_type=F32)


def kernel(
    nrow, ncol,
    tok, lab, gain_one, qkv, proj, table, gain_two, up, down,
    out,
    tok_v, lab_v, g1_v, qkv_v, proj_v, tab_v, g2_v, up_v, down_v,
    beside, corner, top, bot, llab, tlab, ltlab,
    last_all, first_all, last_east, first_east, last_west, first_west,
    ext, branch, groups, wq, wv, wk, gath, bias, bias_s, blocks64, blocks32, scores_v,
    in_sem, send_sem, recv_sem, met_sem,
):
    row, col = lax.axis_index("row"), lax.axis_index("col")
    newest, oldest = col == ncol - 1, col == 0

    def at(dr, dc):
        return (lax.rem(row + dr + nrow, nrow), lax.rem(col + dc + ncol, ncol))

    barrier = pltpu.get_barrier_semaphore()

    def greet(dr, dc):
        pl.semaphore_signal(barrier, inc=1, device_id=at(dr, dc), device_id_type=MESH)

    for dr in (0, 1, -1):
        greet(dr, -1)
        pl.when(jnp.logical_not(newest | (col == ncol - 2)))(functools.partial(greet, dr, 1))
        if dr:
            pl.when(jnp.logical_not(newest))(functools.partial(greet, dr, 0))
    loads = [
        pltpu.make_async_copy(src, dst, in_sem.at[i])
        for i, (src, dst) in enumerate([
            (tok, tok_v), (lab, lab_v), (table, tab_v), (qkv, qkv_v), (gain_one, g1_v),
            (proj, proj_v), (gain_two, g2_v), (up, up_v), (down, down_v),
        ])
    ]
    for load in loads:
        load.start()

    whole = pl.ds(0, 64)
    west, east = pl.ds(0, 4 * C), pl.ds(12 * C, 4 * C)
    moves = [
        (tok.at[whole, east], beside.at[0], (0, 1)),
        (lab, llab, (0, 1)),
        (lab, ltlab, (1, 1)),
        (last_east, corner.at[0, 0], (1, 1)),
        (first_east, corner.at[0, 1], (-1, 1)),
        (last_all, top, (1, 0)),
        (first_all, bot, (-1, 0)),
        (lab, tlab, (1, 0)),
        (tok.at[whole, west], beside.at[1], (0, -1)),
        (last_west, corner.at[1, 0], (1, -1)),
        (first_west, corner.at[1, 1], (-1, -1)),
    ]
    copies = [
        pltpu.make_async_remote_copy(
            src_ref=src, dst_ref=dst, send_sem=send_sem.at[i], recv_sem=recv_sem.at[i],
            device_id=at(*where), device_id_type=MESH,
        )
        for i, (src, dst, where) in enumerate(moves)
    ]
    EAST, ROWS, WEST = range(0, 5), range(5, 8), range(8, 11)

    def send(group):
        for i in group:
            copies[i].start()

    def arrive(group):
        for i in group:
            copies[i].wait_recv()

    def meet(dr):
        pl.semaphore_signal(met_sem, inc=1, device_id=at(dr, 1), device_id_type=MESH)

    @pl.when(newest)
    def _():
        pl.semaphore_wait(barrier, 3)
        send(EAST[:3])
        for dr in (0, 1, -1):
            meet(dr)

    loads[0].wait()

    def pack(rows, high, width, packed):
        rows = rows.astype(F32)
        turned = pltpu.roll(rows, 4, 0)
        low, high = (turned, rows) if high else (rows, turned)
        pieces = []
        for i in range(0, rows.shape[1], 2 * width):
            below = high[:, i + width : i + 2 * width]
            if below.shape[1] == 0:
                below = high[:, i : i + width]
            pieces.append(jnp.where(iota((8, width), 0) < 4, low[:, i : i + width], below))
        packed[...] = jnp.concatenate(pieces, axis=0).astype(BF16)

    foot, crown = tok_v[48:64][8:16], tok_v[0:16][0:8]
    pack(foot[:, 12 * C :], True, 256, last_east)
    pack(crown[:, 12 * C :], False, 256, first_east)

    @pl.when(newest)
    def _():
        send(EAST[3:])

    for load in loads[1:5]:
        load.wait()
    pack(foot, True, 768, last_all)
    pack(crown, False, 768, first_all)
    pack(foot[:, 0 : 4 * C], True, 256, last_west)
    pack(crown[:, 0 : 4 * C], False, 256, first_west)

    eye = (iota((16, 64), 0) == iota((16, 64), 1)).astype(F32)
    apart = jnp.where(iota((64, 64), 0) < 16, (iota((64, 64), 0) != iota((64, 64), 1)).astype(F32) * FAR, 0.0)
    weights = qkv_v[...].astype(F32)
    pad = jnp.zeros((C, 64), F32)
    wq[0:C] = jnp.concatenate([weights[:, 0:C].T, pad], axis=1).astype(BF16)
    wq[C : C + 16] = jnp.concatenate([jnp.zeros((16, C), F32), eye], axis=1).astype(BF16)
    wv[...] = jnp.concatenate([weights[:, 2 * C : 3 * C].T, pad], axis=1).astype(BF16)
    wk[0:C] = jnp.concatenate([weights[:, C : 2 * C], pad], axis=1).astype(BF16)
    wk[C : C + 64] = jnp.concatenate([jnp.zeros((64, C), F32), apart], axis=1).astype(BF16)
    blocks64[...] = jnp.zeros(blocks64.shape, BF16)
    blocks32[...] = jnp.zeros(blocks32.shape, BF16)

    spread = jnp.concatenate([tab_v[...] * LOG2E, jnp.zeros((HEADS, 256 - 225), F32)], axis=1)
    spread = jnp.concatenate([spread, jnp.zeros((8 - HEADS, 256), F32)], axis=0)
    rows = jnp.concatenate([pltpu.roll(spread, 15 * ((s + 4) % 8), 1) if s != 4 else spread for s in range(WIN)], axis=0)
    lane = iota((256, 128), 1)
    select = (iota((256, 128), 0) == ((lane % 8 + 4) % 8 + 7) * 15 + lane // 8).astype(F32)
    gath[...] = jnp.dot(rows, select, precision=lax.Precision.HIGHEST).reshape(8, 8, 128)
    bias_s[...] = jnp.zeros(bias_s.shape, F32)
    for h in range(HEADS):
        strip = gath[:, h, :]
        for x in range(WIN):
            part = strip[:, (7 - x) * 8 : (7 - x) * 8 + 64]
            other = (x + 4) % 8
            bias[x * 8 : x * 8 + 8, h * 64 : h * 64 + 64] = part
            bias_s[1, x * 8 : x * 8 + 8, h * 32 : h * 32 + 32] = part[:, 0:32]
            bias_s[0, other * 8 : other * 8 + 8, h * 32 : h * 32 + 32] = part[:, 32:64]

    gain = g1_v[...].reshape(1, C)
    unit = jnp.ones((C, 128), BF16)

    def mean(values):
        total = dot(values, unit) * (1.0 / C)
        return jnp.concatenate([total, total[:, 0 : C - 128]], axis=1)

    def place(columns, base, start):
        size = columns[0].shape[0]
        tokens = jnp.concatenate(columns, axis=0)
        centred = tokens - mean(tokens.astype(BF16))
        normed = centred * lax.rsqrt(mean((centred * centred).astype(BF16)) + 1e-05) * gain
        for j in range(len(columns)):
            ext[base + j, start : start + size, 0:C] = normed[j * size : j * size + size]

    def split(wide):
        return [wide[:, C * j : C * j + C] for j in range(wide.shape[1] // C)]

    def rim(above, below, base, count):
        above, below = above.astype(F32), below.astype(F32)
        width = above.shape[1]
        parts = []
        for i in range(count * C // width):
            t = i // 2 * 8
            over, under = above[t : t + 8], below[t : t + 8]
            over, under = (over, pltpu.roll(under, 4, 0)) if i % 2 else (pltpu.roll(over, 4, 0), under)
            parts.append(jnp.where(iota((8, width), 0) >= 4, over, under))
        place(split(jnp.concatenate(parts, axis=1)), base, 64)

    def labels_of(above, own):
        above, own = above[...].astype(F32).T, own[...].astype(F32).T
        rows = jnp.concatenate([above[56:64], own], axis=0)
        rows = pltpu.roll(rows.reshape(9, 8, 16), 4, 1).reshape(72, 16)
        spot = iota((72, 1), 0)
        at_end = ((spot < 8) & (row == 0)) | ((spot >= 64) & (row == nrow - 1))
        return rows * 4.0 + jnp.where((spot % 8 < 4) & at_end, 2.0, 0.0)

    def attend(spans, real, nx, column_of, base, table_of, marks, blocks):
        nq = nx * 8
        per = 128 // nq
        wide = -(-HEADS // per)
        heads = [list(range(m * per, min(HEADS, m * per + per))) for m in range(wide)]
        count = len(spans)
        lanes = iota((72, 256), 1)
        pieces = []
        for x in range(WIN):
            value = ext[column_of(x)]
            turned = jnp.concatenate([value[64:72], value[0:64]], axis=0)
            value = jnp.where(iota((72, 256), 0) % 8 < 4, value, turned)
            mark = ((lanes - C).astype(F32) == marks[:, x : x + 1]).astype(F32)
            pieces.append(jnp.where(lanes >= C, mark, value))
        tokens = jnp.concatenate(
            [pieces[x][8 * a : 8 * a + 8] for a in spans[:real] for x in range(WIN)], axis=0
        ).astype(BF16)
        asking = jnp.concatenate(
            [pieces[x][8 * a : 8 * a + 8] for a in spans for x in range(nx)], axis=0
        ).astype(BF16)
        keys = dot(tokens, wk[...]).astype(BF16)
        queries = lax.dot_general(wq[...], asking, NT, preferred_element_type=F32)
        values = lax.dot_general(wv[...], tokens, NT, preferred_element_type=F32)

        block = iota((16, 128), 1) // nq
        block32 = iota((HD, 128), 1) // nq
        for g in range(count // per):
            some = queries[:, 128 * g : 128 * g + 128]
            turns = [some] + [pltpu.roll(some, k * nq, 1) for k in range(1, per)]
            for s in range(min(per, real - per * g)):
                w = per * g + s
                code = turns[(0 - s) % per][C:]
                for t in range(1, per):
                    code = jnp.where(block == t, turns[(t - s) % per][C:], code)
                code = code.astype(BF16)
                for m in range(wide):
                    part = [
                        jnp.where(block32 == h % per, turns[(h - s) % per][h * HD : h * HD + HD], 0.0)
                        for h in heads[m]
                    ]
                    low = heads[m][0] * HD
                    blocks[w, low : low + HD * len(part), 128 * m : 128 * m + 128] = jnp.concatenate(
                        part, axis=0
                    ).astype(BF16)
                    blocks[w, C : C + 16, 128 * m : 128 * m + 128] = code
        table = table_of()
        for w in range(real):
            scores = dot(keys[w * 64 : w * 64 + 64], blocks[w])
            scores_v[w, :, 0 : 128 * wide] = scores * (HD ** (-0.5) * LOG2E) + table
        powers = []
        for w in range(real):
            scores = scores_v[w, :, 0 : 128 * wide]
            powers.append(jnp.exp2(scores - jnp.max(scores, axis=0, keepdims=True)).astype(BF16))
        one = jnp.ones((16, 64), BF16)
        found = []
        for w in range(real):
            mine = values[:, w * 64 : w * 64 + 64].astype(BF16)
            for m in range(wide):
                low, high = heads[m][0] * HD, heads[m][-1] * HD + HD
                sums = dot(jnp.concatenate([mine[low:high], one], axis=0), powers[w][:, 128 * m : 128 * m + 128])
                found.append(sums[0 : high - low] * (1.0 / sums[high - low : high - low + 1]))
        turned = []
        for g in range(count // per):
            rows_of = []
            for h in range(HEADS):
                m, i = h // per, h % per
                row_block = None
                for s in range(min(per, real - per * g)):
                    piece = found[(per * g + s) * wide + m][i * HD : i * HD + HD]
                    if (s - h) % per:
                        piece = pltpu.roll(piece, ((s - h) % per) * nq, 1)
                    row_block = piece if s == 0 else jnp.where(block32 == s, piece, row_block)
                rows_of.append(row_block)
            turned.append(jnp.concatenate(rows_of, axis=0))
        attended = jnp.concatenate(turned, axis=1).T.astype(BF16)
        mixed = dot(attended, proj_v[...])
        for w, a in enumerate(spans[:real]):
            for x in range(nx):
                spot = w * nq + x * 8
                branch[base + x, 8 * a : 8 * a + 8] = mixed[spot : spot + 8]

    def finish(f, size):
        lanes = pl.ds(f * 768 if isinstance(f, int) else pl.multiple_of(f * 768, 768), size * C)
        columns = split(tok_v[:, lanes].astype(F32))
        upper = iota((64, C), 0) % 8 < 4
        residual = jnp.concatenate(
            [
                columns[j] + jnp.where(upper, branch[4 * f + j, 0:64], branch[4 * f + j, 8:72])
                for j in range(size)
            ],
            axis=0,
        )
        high = residual.astype(BF16)
        low = (residual - high.astype(F32)).astype(BF16)
        centred = residual - (mean(high) + mean(low))
        variance = mean((centred * centred).astype(BF16))
        second = (centred * lax.rsqrt(variance + 1e-05) * g2_v[...].reshape(1, C)).astype(BF16)
        hidden = dot(second, up_v[...])
        square = hidden * hidden
        logit = LOGIT[6] * square + LOGIT[5]
        for k in range(4, -1, -1):
            logit = logit * square + LOGIT[k]
        hidden = (hidden * (1.0 / (1.0 + jnp.exp2(hidden * logit)))).astype(BF16)
        done = residual + lax.dot_general(hidden, down_v[...], NT, preferred_element_type=F32)
        out[:, lanes] = jnp.concatenate([done[j * 64 : j * 64 + 64] for j in range(size)], axis=1).astype(BF16)

    place(split(tok_v[...].astype(F32)), 4, 0)

    @pl.when(jnp.logical_not(newest))
    def _():
        pl.semaphore_wait(barrier, jnp.where(oldest, 5, 8))
        send(EAST)
        send(ROWS)
        pl.when(jnp.logical_not(oldest))(functools.partial(send, WEST))
        pl.when(col == ncol - 2)(functools.partial(meet, 0))

    loads[5].wait()
    attend([1, 2, 3, 4, 5, 6, 7, 7], 7, 8, lambda x: 8 + x, 4, lambda: bias[...], labels_of(lab_v, lab_v), blocks64)

    @pl.when(newest)
    def _():
        pl.semaphore_wait(met_sem, 1)
        send(ROWS)
        send(WEST)

    arrive(ROWS)
    marks = labels_of(tlab, lab_v)
    place_x = iota((72, 8), 1)
    groups[1] = marks[:, 8:16] + jnp.where((place_x >= 4) & newest, 1.0, 0.0)
    rim(top[...], bot[...], 4, 16)
    attend([0, 8], 2, 8, lambda x: 8 + x, 4, lambda: bias[...], marks, blocks64)
    for load in loads[6:]:
        load.wait()
    finish(1, 8)

    def edge(i, carry):
        side = jnp.where(newest, i, 1 - i)

        @pl.when(side == 1)
        def _():
            arrive(WEST)

        @pl.when((side == 0) & oldest)
        def _():
            pl.semaphore_wait(met_sem, 3)
            send(WEST)

        @pl.when(side == 0)
        def _():
            arrive(EAST)
            near = labels_of(ltlab, llab)
            near = jnp.concatenate([near[:, 12:16], near[:, 8:12]], axis=1)
            groups[0] = near + jnp.where((place_x < 4) & oldest, 1.0, 0.0)

        place(split(beside[side].astype(F32)), 20 * side, 0)
        rim(corner[side, 0], corner[side, 1], 20 * side, 4)
        attend(
            list(range(9)) + [8] * 3, 9, 4,
            lambda x: 16 * side + x + (1 - side) * (4 if x < 4 else -4),
            12 * side, lambda: bias_s[side], groups[side], blocks32,
        )
        finish(3 * side, 4)
        return carry

    lax.fori_loop(0, 2, edge, 0)
    for copy in copies:
        copy.wait_send()


def local(nrow, ncol, tok, lab, gain_one, qkv, proj, table, gain_two, up, down):
    args = (tok, lab.T, gain_one, qkv, proj, table, gain_two, up, down.T)
    vmem = pltpu.VMEM
    scratch = [vmem(a.shape, a.dtype) for a in args]
    args = [pltpu.with_memory_space_constraint(a, pltpu.HBM) for a in args]
    scratch += [vmem((2, 64, 768), BF16), vmem((2, 2, 16, 256), BF16)] + [vmem((16, 768), BF16)] * 2
    scratch += [vmem((16, 64), jnp.int32)] * 3
    scratch += [vmem((16, 768), BF16)] * 2 + [vmem((16, 256), BF16)] * 4
    scratch += [vmem((24, 72, 256), F32), vmem((16, 72, C), F32), vmem((2, 72, 8), F32)]
    scratch += [vmem((C + 16, 256), BF16), vmem((C, 256), BF16), vmem((256, 256), BF16)]
    scratch += [vmem((8, 8, 128), F32), vmem((64, 384), F32), vmem((2, 64, 256), F32)]
    scratch += [vmem((10, 256, 384), BF16), vmem((12, 256, 256), BF16), vmem((12, 64, 384), F32)]
    scratch += [pltpu.SemaphoreType.DMA((9,)), pltpu.SemaphoreType.DMA((11,)), pltpu.SemaphoreType.DMA((11,))]
    scratch += [pltpu.SemaphoreType.REGULAR]
    return pl.pallas_call(
        functools.partial(kernel, nrow, ncol),
        out_shape=vmem((64, 3072), BF16),
        in_specs=[pl.BlockSpec(memory_space=pltpu.HBM)] * len(args),
        out_specs=pl.BlockSpec(memory_space=vmem),
        scratch_shapes=scratch,
        compiler_params=pltpu.CompilerParams(
            collective_id=0, has_side_effects=True, vmem_limit_bytes=56 * 1024 * 1024
        ),
        name="window_block",
    )(*args)


def solution(mesh):
    placed = (P("row", "col"), P("row", "col"), P(), P(), P(), P(), P(), P(), P())
    return jax.shard_map(
        functools.partial(local, mesh.shape["row"], mesh.shape["col"]),
        mesh=mesh, in_specs=placed, out_specs=P("row", "col"), check_vma=False,
    )
```

```python
import functools

import jax
import jax.numpy as jnp
from jax import lax
from jax.experimental import pallas as pl
from jax.experimental.pallas import tpu as pltpu
from jax.sharding import PartitionSpec as P

C = 192
HEADS = 6
HID = 768
WIN = 8
HD = 32
MESH = pl.DeviceIdType.MESH
F32 = jnp.float32
BF16 = jnp.bfloat16
LOG2E = 1.4426950408889634
FAR = -1e30
NT = (((1,), (1,)), ((), ()))
LOGIT = (
    -2.3022072315216064, -0.10483857989311218, 9.559292084304616e-05, 0.00015938941214699298,
    -1.1452430044300854e-05, 3.8504501276293013e-07, -5.209909392789314e-09,
)


def iota(shape, axis):
    return lax.broadcasted_iota(jnp.int32, shape, axis)


def dot(a, b):
    return jnp.dot(a, b, preferred_element_type=F32)


def in_pieces(step, apply, *arrays):
    return jnp.concatenate(
        [apply(*(a[i : i + step] for a in arrays)) for i in range(0, arrays[0].shape[0], step)], axis=0
    )


def gelu(v):
    square = v * v
    logit = LOGIT[6] * square + LOGIT[5]
    for k in range(4, -1, -1):
        logit = logit * square + LOGIT[k]
    return (v * (1.0 / (1.0 + jnp.exp2(v * logit)))).astype(BF16)


def kernel(
    nrow, ncol,
    tok, lab, gain_one, qkv, proj, table, gain_two, up, down,
    out,
    tok_v, lab_v, g1_v, qkv_v, proj_v, tab_v, g2_v, up_v, down_v,
    beside, corner, top, bot, llab, tlab, ltlab,
    last_all, first_all,
    ext, branch, groups, wq, wv, wk, gath, bias, bias_s, blocks64, blocks32, scores_v,
    in_sem, send_sem, recv_sem, met_sem, first_sem,
):
    row, col = lax.axis_index("row"), lax.axis_index("col")
    newest, oldest = col == ncol - 1, col == 0
    corner_row = (row <= 1) | (row == nrow - 1)
    first = (row == 0) & oldest
    near_first = corner_row & (col <= 1) & jnp.logical_not(first)
    early = newest | first

    def at(dr, dc):
        return (lax.rem(row + dr + nrow, nrow), lax.rem(col + dc + ncol, ncol))

    barrier = pltpu.get_barrier_semaphore()

    def greet(dr, dc):
        pl.semaphore_signal(barrier, inc=1, device_id=at(dr, dc), device_id_type=MESH)

    for dr in (0, 1, -1):
        greet(dr, -1)
    expected = jnp.where(newest, 3, jnp.where(oldest, 5, 8)) - near_first.astype(jnp.int32)
    foot, crown, waist = pl.ds(48, 16), pl.ds(0, 16), pl.ds(16, 32)
    whole = pl.ds(0, 64)
    west, east = pl.ds(0, 4 * C), pl.ds(12 * C, 4 * C)
    moves = [
        (tok.at[foot, east], corner.at[0, 0], (1, 1)),
        (tok.at[crown, east], corner.at[0, 1], (-1, 1)),
        (lab, ltlab, (1, 1)),
        (lab, llab, (0, 1)),
        (tok.at[whole, east], beside.at[0], (0, 1)),
        (last_all, top, (1, 0)),
        (first_all, bot, (-1, 0)),
        (lab, tlab, (1, 0)),
        (tok.at[foot, west], corner.at[1, 0], (1, -1)),
        (tok.at[crown, west], corner.at[1, 1], (-1, -1)),
        (tok.at[whole, west], beside.at[1], (0, -1)),
    ]
    copies = [
        pltpu.make_async_remote_copy(
            src_ref=src, dst_ref=dst, send_sem=send_sem.at[i], recv_sem=recv_sem.at[i],
            device_id=at(*where), device_id_type=MESH,
        )
        for i, (src, dst, where) in enumerate(moves)
    ]
    EAST, ROWS, WEST = range(0, 5), range(5, 8), range(8, 11)

    def send(group):
        for i in group:
            copies[i].start()

    def send_but_first(group):
        for i in group:
            dr, dc = moves[i][2]
            to = at(dr, dc)
            pl.when((to[0] != 0) | (to[1] != 0))(copies[i].start)

    def send_first(group):
        for i in group:
            dr, dc = moves[i][2]
            to = at(dr, dc)
            pl.when((to[0] == 0) & (to[1] == 0))(copies[i].start)

    def arrive(group):
        for i in group:
            copies[i].wait_recv()

    def meet(dr):
        pl.semaphore_signal(met_sem, inc=1, device_id=at(dr, 1), device_id_type=MESH)

    @pl.when(early)
    def _():
        pl.semaphore_wait(barrier, expected)
        send(EAST)

        @pl.when(newest)
        def _():
            for dr in (0, 1, -1):
                meet(dr)

        @pl.when(first)
        def _():
            for dr, dc in ((1, 0), (-1, 0), (0, 1), (1, 1), (-1, 1)):
                pl.semaphore_signal(first_sem, inc=1, device_id=at(dr, dc), device_id_type=MESH)

    for dr in (0, 1, -1):
        pl.when(jnp.logical_not(newest | (col == ncol - 2) | first))(functools.partial(greet, dr, 1))
        if dr:
            pl.when(jnp.logical_not(newest | first))(functools.partial(greet, dr, 0))
    loads = [
        pltpu.make_async_copy(src, dst, in_sem.at[i])
        for i, (src, dst) in enumerate([
            (tok.at[foot], tok_v.at[foot]), (tok.at[crown], tok_v.at[crown]), (tok.at[waist], tok_v.at[waist]),
            (lab, lab_v), (table, tab_v), (qkv, qkv_v), (gain_one, g1_v),
            (proj, proj_v), (gain_two, g2_v), (up, up_v), (down, down_v),
        ])
    ]
    for load in loads:
        load.start()

    loads[0].wait()
    loads[1].wait()

    def pack(rows, high, width, packed):
        rows = rows.astype(F32)
        turned = pltpu.roll(rows, 4, 0)
        low, high = (turned, rows) if high else (rows, turned)
        pieces = []
        for i in range(0, rows.shape[1], 2 * width):
            below = high[:, i + width : i + 2 * width]
            if below.shape[1] == 0:
                below = high[:, i : i + width]
            pieces.append(jnp.where(iota((8, width), 0) < 4, low[:, i : i + width], below))
        packed[...] = jnp.concatenate(pieces, axis=0).astype(BF16)

    pack(tok_v[48:64][8:16], True, 768, last_all)
    pack(tok_v[0:16][0:8], False, 768, first_all)
    pl.when(first)(functools.partial(send, ROWS))
    for load in loads[2:7]:
        load.wait()

    eye = (iota((16, 64), 0) == iota((16, 64), 1)).astype(F32)
    apart = jnp.where(iota((64, 64), 0) < 16, (iota((64, 64), 0) != iota((64, 64), 1)).astype(F32) * FAR, 0.0)
    weights = qkv_v[...].astype(F32)
    pad = jnp.zeros((C, 64), F32)
    wq[0:C] = jnp.concatenate([weights[:, 0:C].T, pad], axis=1).astype(BF16)
    wq[C : C + 16] = jnp.concatenate([jnp.zeros((16, C), F32), eye], axis=1).astype(BF16)
    wv[...] = jnp.concatenate([weights[:, 2 * C : 3 * C].T, pad], axis=1).astype(BF16)
    wk[0:C] = jnp.concatenate([weights[:, C : 2 * C], pad], axis=1).astype(BF16)
    wk[C : C + 64] = jnp.concatenate([jnp.zeros((64, C), F32), apart], axis=1).astype(BF16)
    blocks64[...] = jnp.zeros(blocks64.shape, BF16)
    blocks32[...] = jnp.zeros(blocks32.shape, BF16)

    spread = jnp.concatenate([tab_v[...] * LOG2E, jnp.zeros((HEADS, 256 - 225), F32)], axis=1)
    spread = jnp.concatenate([spread, jnp.zeros((8 - HEADS, 256), F32)], axis=0)
    rows = jnp.concatenate([pltpu.roll(spread, 15 * ((s + 4) % 8), 1) if s != 4 else spread for s in range(WIN)], axis=0)
    lane = iota((256, 128), 1)
    select = (iota((256, 128), 0) == ((lane % 8 + 4) % 8 + 7) * 15 + lane // 8).astype(F32)
    gath[...] = jnp.dot(rows, select, precision=lax.Precision.HIGHEST).reshape(8, 8, 128)
    bias_s[...] = jnp.zeros(bias_s.shape, F32)
    for h in range(HEADS):
        strip = gath[:, h, :]
        for x in range(WIN):
            part = strip[:, (7 - x) * 8 : (7 - x) * 8 + 64]
            other = (x + 4) % 8
            bias[x * 8 : x * 8 + 8, h * 64 : h * 64 + 64] = part
            bias_s[1, x * 8 : x * 8 + 8, h * 32 : h * 32 + 32] = part[:, 0:32]
            bias_s[0, other * 8 : other * 8 + 8, h * 32 : h * 32 + 32] = part[:, 32:64]

    gain = g1_v[...].reshape(1, C)
    unit = jnp.ones((C, 128), BF16)

    def mean(values):
        total = dot(values, unit) * (1.0 / C)
        return jnp.concatenate([total, total[:, 0 : C - 128]], axis=1)

    def place(columns, base, start):
        size = columns[0].shape[0]
        tokens = jnp.concatenate(columns, axis=0)
        centred = tokens - mean(tokens.astype(BF16))
        normed = centred * lax.rsqrt(mean((centred * centred).astype(BF16)) + 1e-05) * gain
        for j in range(len(columns)):
            ext[base + j, start : start + size, 0:C] = normed[j * size : j * size + size]

    def split(wide):
        return [wide[:, C * j : C * j + C] for j in range(wide.shape[1] // C)]

    def rim(above, below):
        return split(jnp.where(iota(above.shape, 0) >= 4, above, below))

    def unpack(packed, high):
        packed = packed.astype(F32)
        pieces = []
        for i in range(4):
            piece = packed[i // 2 * 8 : i // 2 * 8 + 8]
            pieces.append(pltpu.roll(piece, 4, 0) if (i % 2 == 1) != high else piece)
        return jnp.concatenate(pieces, axis=1)

    def labels_of(above, own):
        above, own = above[...].astype(F32).T, own[...].astype(F32).T
        rows = jnp.concatenate([above[56:64], own], axis=0)
        rows = pltpu.roll(rows.reshape(9, 8, 16), 4, 1).reshape(72, 16)
        spot = iota((72, 1), 0)
        at_end = ((spot < 8) & (row == 0)) | ((spot >= 64) & (row == nrow - 1))
        return rows * 4.0 + jnp.where((spot % 8 < 4) & at_end, 2.0, 0.0)

    def attend(spans, real, nx, column_of, base, table_of, marks, blocks):
        nq = nx * 8
        per = 128 // nq
        wide = -(-HEADS // per)
        heads = [list(range(m * per, min(HEADS, m * per + per))) for m in range(wide)]
        count = len(spans)
        lanes = iota((72, 256), 1)
        pieces = []
        for x in range(WIN):
            value = ext[column_of(x)]
            turned = jnp.concatenate([value[64:72], value[0:64]], axis=0)
            value = jnp.where(iota((72, 256), 0) % 8 < 4, value, turned)
            mark = ((lanes - C).astype(F32) == marks[:, x : x + 1]).astype(F32)
            pieces.append(jnp.where(lanes >= C, mark, value))
        tokens = jnp.concatenate(
            [pieces[x][8 * a : 8 * a + 8] for a in spans[:real] for x in range(WIN)], axis=0
        ).astype(BF16)
        asking = jnp.concatenate(
            [pieces[x][8 * a : 8 * a + 8] for a in spans for x in range(nx)], axis=0
        ).astype(BF16)
        keys = dot(tokens, wk[...]).astype(BF16)
        queries = lax.dot_general(wq[...], asking, NT, preferred_element_type=F32)
        values = lax.dot_general(wv[...], tokens, NT, preferred_element_type=F32)

        block = iota((16, 128), 1) // nq
        block32 = iota((HD, 128), 1) // nq
        for g in range(count // per):
            some = queries[:, 128 * g : 128 * g + 128]
            turns = [some] + [pltpu.roll(some, k * nq, 1) for k in range(1, per)]
            for s in range(min(per, real - per * g)):
                w = per * g + s
                code = turns[(0 - s) % per][C:]
                for t in range(1, per):
                    code = jnp.where(block == t, turns[(t - s) % per][C:], code)
                code = code.astype(BF16)
                for m in range(wide):
                    part = [
                        jnp.where(block32 == h % per, turns[(h - s) % per][h * HD : h * HD + HD], 0.0)
                        for h in heads[m]
                    ]
                    low = heads[m][0] * HD
                    blocks[w, low : low + HD * len(part), 128 * m : 128 * m + 128] = jnp.concatenate(
                        part, axis=0
                    ).astype(BF16)
                    blocks[w, C : C + 16, 128 * m : 128 * m + 128] = code
        table = table_of()
        for w in range(real):
            scores = dot(keys[w * 64 : w * 64 + 64], blocks[w])
            scores_v[w, :, 0 : 128 * wide] = scores * (HD ** (-0.5) * LOG2E) + table
        powers = []
        for w in range(real):
            scores = scores_v[w, :, 0 : 128 * wide]
            powers.append(jnp.exp2(scores - jnp.max(scores, axis=0, keepdims=True)).astype(BF16))
        one = jnp.ones((16, 64), BF16)
        found = []
        for w in range(real):
            mine = values[:, w * 64 : w * 64 + 64].astype(BF16)
            for m in range(wide):
                low, high = heads[m][0] * HD, heads[m][-1] * HD + HD
                sums = dot(jnp.concatenate([mine[low:high], one], axis=0), powers[w][:, 128 * m : 128 * m + 128])
                found.append(sums[0 : high - low] * (1.0 / sums[high - low : high - low + 1]))
        turned = []
        for g in range(count // per):
            rows_of = []
            for h in range(HEADS):
                m, i = h // per, h % per
                row_block = None
                for s in range(min(per, real - per * g)):
                    piece = found[(per * g + s) * wide + m][i * HD : i * HD + HD]
                    if (s - h) % per:
                        piece = pltpu.roll(piece, ((s - h) % per) * nq, 1)
                    row_block = piece if s == 0 else jnp.where(block32 == s, piece, row_block)
                rows_of.append(row_block)
            turned.append(jnp.concatenate(rows_of, axis=0))
        attended = jnp.concatenate(turned, axis=1).astype(BF16).T
        mixed = dot(attended, proj_v[...])
        for w, a in enumerate(spans[:real]):
            for x in range(nx):
                spot = w * nq + x * 8
                branch[base + x, 8 * a : 8 * a + 8] = mixed[spot : spot + 8]

    def finish(f, size):
        lanes = pl.ds(f * 768 if isinstance(f, int) else pl.multiple_of(f * 768, 768), size * C)
        columns = split(tok_v[:, lanes].astype(F32))
        upper = iota((64, C), 0) % 8 < 4
        residual = jnp.concatenate(
            [
                columns[j] + jnp.where(upper, branch[4 * f + j, 0:64], branch[4 * f + j, 8:72])
                for j in range(size)
            ],
            axis=0,
        )
        high = residual.astype(BF16)
        low = (residual - high.astype(F32)).astype(BF16)
        centred = residual - (mean(high) + mean(low))
        variance = mean((centred * centred).astype(BF16))
        second = (centred * lax.rsqrt(variance + 1e-05) * g2_v[...].reshape(1, C)).astype(BF16)
        done = residual
        for n in range(0, HID, 256):
            hidden = in_pieces(32, gelu, dot(second, up_v[:, n : n + 256]))
            done = done + lax.dot_general(hidden, down_v[:, n : n + 256], NT, preferred_element_type=F32)
        out[:, lanes] = jnp.concatenate([done[j * 64 : j * 64 + 64] for j in range(size)], axis=1).astype(BF16)

    place(split(tok_v[...].astype(F32)), 4, 0)

    @pl.when(jnp.logical_not(early))
    def _():
        pl.semaphore_wait(barrier, expected)
        pl.when(col == ncol - 2)(functools.partial(meet, 0))
        send_but_first(ROWS)
        send(EAST)
        pl.when(jnp.logical_not(oldest))(functools.partial(send_but_first, WEST))

    loads[7].wait()
    attend([1, 2, 3, 4, 5, 6, 7, 7], 7, 8, lambda x: 8 + x, 4, lambda: bias[...], labels_of(lab_v, lab_v), blocks64)

    @pl.when(newest)
    def _():
        pl.semaphore_wait(met_sem, 1)
        send(ROWS)
        send(WEST)

    @pl.when(near_first)
    def _():
        pl.semaphore_wait(first_sem, 1)
        pl.when(oldest)(functools.partial(send_first, ROWS))
        pl.when(jnp.logical_not(oldest))(functools.partial(send_first, WEST))

    arrive(ROWS)
    marks = labels_of(tlab, lab_v)
    place_x = iota((72, 8), 1)
    groups[1] = marks[:, 8:16] + jnp.where((place_x >= 4) & newest, 1.0, 0.0)
    place(rim(unpack(top[...], True), unpack(bot[...], False)), 4, 64)
    attend([0, 8], 2, 8, lambda x: 8 + x, 4, lambda: bias[...], marks, blocks64)
    for load in loads[8:]:
        load.wait()
    finish(1, 8)

    def edge(i, carry):
        side = jnp.where(oldest, 1 - i, i)

        @pl.when(side == 1)
        def _():
            arrive(WEST)

        @pl.when((side == 0) & oldest)
        def _():
            pl.semaphore_wait(met_sem, 3)
            send(WEST)

        @pl.when(side == 0)
        def _():
            arrive(EAST[2:4])
            near = labels_of(ltlab, llab)
            near = jnp.concatenate([near[:, 12:16], near[:, 8:12]], axis=1)
            groups[0] = near + jnp.where((place_x < 4) & oldest, 1.0, 0.0)
            arrive(EAST[0:2])
            arrive(EAST[4:5])

        edges = rim(corner[side, 0].astype(F32)[8:16], corner[side, 1].astype(F32)[0:8])
        near = split(beside[side].astype(F32))
        place([jnp.concatenate(pair, axis=0) for pair in zip(near, edges)], 20 * side, 0)
        attend(
            list(range(9)) + [8] * 3, 9, 4,
            lambda x: 16 * side + x + (1 - side) * (4 if x < 4 else -4),
            12 * side, lambda: bias_s[side], groups[side], blocks32,
        )
        finish(3 * side, 4)
        return carry

    lax.fori_loop(0, 2, edge, 0)
    for copy in copies:
        copy.wait_send()


def local(nrow, ncol, tok, lab, gain_one, qkv, proj, table, gain_two, up, down):
    args = (tok, lab.T, gain_one, qkv, proj, table, gain_two, up, down.T)
    vmem = pltpu.VMEM
    scratch = [vmem(a.shape, a.dtype) for a in args]
    args = [pltpu.with_memory_space_constraint(a, pltpu.HBM) for a in args]
    scratch += [vmem((2, 64, 768), BF16), vmem((2, 2, 16, 768), BF16)] + [vmem((16, 768), BF16)] * 2
    scratch += [vmem((16, 64), jnp.int32)] * 3
    scratch += [vmem((16, 768), BF16)] * 2
    scratch += [vmem((24, 72, 256), F32), vmem((16, 72, C), F32), vmem((2, 72, 8), F32)]
    scratch += [vmem((C + 16, 256), BF16), vmem((C, 256), BF16), vmem((256, 256), BF16)]
    scratch += [vmem((8, 8, 128), F32), vmem((64, 384), F32), vmem((2, 64, 256), F32)]
    scratch += [vmem((10, 256, 384), BF16), vmem((12, 256, 256), BF16), vmem((12, 64, 384), F32)]
    scratch += [pltpu.SemaphoreType.DMA((11,)), pltpu.SemaphoreType.DMA((11,)), pltpu.SemaphoreType.DMA((11,))]
    scratch += [pltpu.SemaphoreType.REGULAR] * 2
    return pl.pallas_call(
        functools.partial(kernel, nrow, ncol),
        out_shape=vmem((64, 3072), BF16),
        in_specs=[pl.BlockSpec(memory_space=pltpu.HBM)] * len(args),
        out_specs=pl.BlockSpec(memory_space=vmem),
        scratch_shapes=scratch,
        compiler_params=pltpu.CompilerParams(
            collective_id=0, has_side_effects=True, vmem_limit_bytes=56 * 1024 * 1024
        ),
        name="window_block",
    )(*args)


def solution(mesh):
    placed = (P("row", "col"), P("row", "col"), P(), P(), P(), P(), P(), P(), P())
    return jax.shard_map(
        functools.partial(local, mesh.shape["row"], mesh.shape["col"]),
        mesh=mesh, in_specs=placed, out_specs=P("row", "col"), check_vma=False,
    )
```

```python
import functools

import jax
import jax.numpy as jnp
from jax import lax
from jax.experimental import pallas as pl
from jax.experimental.pallas import tpu as pltpu
from jax.sharding import PartitionSpec as P

C = 192
HEADS = 6
HID = 768
WIN = 8
HD = 32
MESH = pl.DeviceIdType.MESH
F32 = jnp.float32
BF16 = jnp.bfloat16
LOG2E = 1.4426950408889634
FAR = -1e30
NT = (((1,), (1,)), ((), ()))
LOGIT = (
    -2.3022072315216064, -0.10483857989311218, 9.559292084304616e-05, 0.00015938941214699298,
    -1.1452430044300854e-05, 3.8504501276293013e-07, -5.209909392789314e-09,
)


def iota(shape, axis):
    return lax.broadcasted_iota(jnp.int32, shape, axis)


def dot(a, b):
    return jnp.dot(a, b, preferred_element_type=F32)


def in_pieces(step, apply, *arrays):
    return jnp.concatenate(
        [apply(*(a[i : i + step] for a in arrays)) for i in range(0, arrays[0].shape[0], step)], axis=0
    )


def gelu(v):
    square = v * v
    logit = LOGIT[6] * square + LOGIT[5]
    for k in range(4, -1, -1):
        logit = logit * square + LOGIT[k]
    return (v * (1.0 / (1.0 + jnp.exp2(v * logit)))).astype(BF16)


def kernel(
    nrow, ncol,
    tok, lab, gain_one, qkv, proj, table, gain_two, up, down,
    out,
    tok_v, lab_v, g1_v, qkv_v, proj_v, tab_v, g2_v, up_v, down_v,
    beside, corner, top, bot, llab, tlab, ltlab,
    last_all, first_all, last_east, first_east, last_west, first_west,
    ext, branch, groups, wq, wv, wk, gath, bias, bias_s, blocks64, blocks32, scores_v,
    in_sem, send_sem, recv_sem, met_sem, first_sem,
):
    row, col = lax.axis_index("row"), lax.axis_index("col")
    newest, oldest = col == ncol - 1, col == 0
    corner_row = (row <= 1) | (row == nrow - 1)
    first = (row == 0) & oldest
    near_first = corner_row & (col <= 1) & jnp.logical_not(first)
    early = newest | first

    def at(dr, dc):
        return (lax.rem(row + dr + nrow, nrow), lax.rem(col + dc + ncol, ncol))

    barrier = pltpu.get_barrier_semaphore()

    def greet(dr, dc):
        pl.semaphore_signal(barrier, inc=1, device_id=at(dr, dc), device_id_type=MESH)

    for dr in (0, 1, -1):
        greet(dr, -1)
    expected = jnp.where(newest, 3, jnp.where(oldest, 5, 8)) - near_first.astype(jnp.int32)
    foot, crown, waist = pl.ds(48, 16), pl.ds(0, 16), pl.ds(16, 32)
    whole = pl.ds(0, 64)
    west, east = pl.ds(0, 4 * C), pl.ds(12 * C, 4 * C)
    moves = [
        (last_east, corner.at[0, 0], (1, 1)),
        (first_east, corner.at[0, 1], (-1, 1)),
        (lab, ltlab, (1, 1)),
        (lab, llab, (0, 1)),
        (tok.at[whole, east], beside.at[0], (0, 1)),
        (last_all, top, (1, 0)),
        (first_all, bot, (-1, 0)),
        (lab, tlab, (1, 0)),
        (last_west, corner.at[1, 0], (1, -1)),
        (first_west, corner.at[1, 1], (-1, -1)),
        (tok.at[whole, west], beside.at[1], (0, -1)),
    ]
    copies = [
        pltpu.make_async_remote_copy(
            src_ref=src, dst_ref=dst, send_sem=send_sem.at[i], recv_sem=recv_sem.at[i],
            device_id=at(*where), device_id_type=MESH,
        )
        for i, (src, dst, where) in enumerate(moves)
    ]
    EAST, ROWS, WEST = range(0, 5), range(5, 8), range(8, 11)

    def send(group):
        for i in group:
            copies[i].start()

    def send_but_first(group):
        for i in group:
            dr, dc = moves[i][2]
            to = at(dr, dc)
            pl.when((to[0] != 0) | (to[1] != 0))(copies[i].start)

    def send_first(group):
        for i in group:
            dr, dc = moves[i][2]
            to = at(dr, dc)
            pl.when((to[0] == 0) & (to[1] == 0))(copies[i].start)

    def arrive(group):
        for i in group:
            copies[i].wait_recv()

    def meet(dr):
        pl.semaphore_signal(met_sem, inc=1, device_id=at(dr, 1), device_id_type=MESH)

    def pack(rows, high, width, packed):
        rows = rows.astype(F32)
        turned = pltpu.roll(rows, 4, 0)
        low, high = (turned, rows) if high else (rows, turned)
        pieces = []
        for i in range(0, rows.shape[1], 2 * width):
            below = high[:, i + width : i + 2 * width]
            if below.shape[1] == 0:
                below = high[:, i : i + width]
            pieces.append(jnp.where(iota((8, width), 0) < 4, low[:, i : i + width], below))
        packed[...] = jnp.concatenate(pieces, axis=0).astype(BF16)

    edges = [
        pltpu.make_async_copy(tok.at[rows, east], tok_v.at[rows, east], in_sem.at[11 + i])
        for i, rows in enumerate((foot, crown))
    ]

    @pl.when(early)
    def _():
        pl.semaphore_wait(barrier, expected)
        for edge in edges:
            edge.start()
        for edge in edges:
            edge.wait()
        pack(tok_v[48:64, 12 * C :][8:16], True, 256, last_east)
        pack(tok_v[0:16, 12 * C :][0:8], False, 256, first_east)
        send(EAST)

        @pl.when(newest)
        def _():
            for dr in (0, 1, -1):
                meet(dr)

        @pl.when(first)
        def _():
            for dr, dc in ((1, 0), (-1, 0), (0, 1), (1, 1), (-1, 1)):
                pl.semaphore_signal(first_sem, inc=1, device_id=at(dr, dc), device_id_type=MESH)

    for dr in (0, 1, -1):
        pl.when(jnp.logical_not(newest | (col == ncol - 2) | first))(functools.partial(greet, dr, 1))
        if dr:
            pl.when(jnp.logical_not(newest | first))(functools.partial(greet, dr, 0))
    loads = [
        pltpu.make_async_copy(src, dst, in_sem.at[i])
        for i, (src, dst) in enumerate([
            (tok.at[foot], tok_v.at[foot]), (tok.at[crown], tok_v.at[crown]), (tok.at[waist], tok_v.at[waist]),
            (lab, lab_v), (table, tab_v), (qkv, qkv_v), (gain_one, g1_v),
            (proj, proj_v), (gain_two, g2_v), (up, up_v), (down, down_v),
        ])
    ]
    for load in loads:
        load.start()

    loads[0].wait()
    loads[1].wait()

    pack(tok_v[48:64][8:16], True, 768, last_all)
    pack(tok_v[0:16][0:8], False, 768, first_all)
    pack(tok_v[48:64, 0 : 4 * C][8:16], True, 256, last_west)
    pack(tok_v[0:16, 0 : 4 * C][0:8], False, 256, first_west)

    @pl.when(jnp.logical_not(early))
    def _():
        pack(tok_v[48:64, 12 * C :][8:16], True, 256, last_east)
        pack(tok_v[0:16, 12 * C :][0:8], False, 256, first_east)

    pl.when(first)(functools.partial(send, ROWS))
    for load in loads[2:7]:
        load.wait()

    eye = (iota((16, 64), 0) == iota((16, 64), 1)).astype(F32)
    apart = jnp.where(iota((64, 64), 0) < 16, (iota((64, 64), 0) != iota((64, 64), 1)).astype(F32) * FAR, 0.0)
    weights = qkv_v[...].astype(F32)
    pad = jnp.zeros((C, 64), F32)
    wq[0:C] = jnp.concatenate([weights[:, 0:C].T, pad], axis=1).astype(BF16)
    wq[C : C + 16] = jnp.concatenate([jnp.zeros((16, C), F32), eye], axis=1).astype(BF16)
    wv[...] = jnp.concatenate([weights[:, 2 * C : 3 * C].T, pad], axis=1).astype(BF16)
    wk[0:C] = jnp.concatenate([weights[:, C : 2 * C], pad], axis=1).astype(BF16)
    wk[C : C + 64] = jnp.concatenate([jnp.zeros((64, C), F32), apart], axis=1).astype(BF16)
    blocks64[...] = jnp.zeros(blocks64.shape, BF16)
    blocks32[...] = jnp.zeros(blocks32.shape, BF16)

    spread = jnp.concatenate([tab_v[...] * LOG2E, jnp.zeros((HEADS, 256 - 225), F32)], axis=1)
    spread = jnp.concatenate([spread, jnp.zeros((8 - HEADS, 256), F32)], axis=0)
    rows = jnp.concatenate([pltpu.roll(spread, 15 * ((s + 4) % 8), 1) if s != 4 else spread for s in range(WIN)], axis=0)
    lane = iota((256, 128), 1)
    select = (iota((256, 128), 0) == ((lane % 8 + 4) % 8 + 7) * 15 + lane // 8).astype(F32)
    gath[...] = jnp.dot(rows, select, precision=lax.Precision.HIGHEST).reshape(8, 8, 128)
    bias_s[...] = jnp.zeros(bias_s.shape, F32)
    for h in range(HEADS):
        strip = gath[:, h, :]
        for x in range(WIN):
            part = strip[:, (7 - x) * 8 : (7 - x) * 8 + 64]
            other = (x + 4) % 8
            bias[x * 8 : x * 8 + 8, h * 64 : h * 64 + 64] = part
            bias_s[1, x * 8 : x * 8 + 8, h * 32 : h * 32 + 32] = part[:, 0:32]
            bias_s[0, other * 8 : other * 8 + 8, h * 32 : h * 32 + 32] = part[:, 32:64]

    gain = g1_v[...].reshape(1, C)
    unit = jnp.ones((C, 128), BF16)

    def mean(values):
        total = dot(values, unit) * (1.0 / C)
        return jnp.concatenate([total, total[:, 0 : C - 128]], axis=1)

    def place(columns, base, start):
        size = columns[0].shape[0]
        tokens = jnp.concatenate(columns, axis=0)
        centred = tokens - mean(tokens.astype(BF16))
        normed = centred * lax.rsqrt(mean((centred * centred).astype(BF16)) + 1e-05) * gain
        for j in range(len(columns)):
            ext[base + j, start : start + size, 0:C] = normed[j * size : j * size + size]

    def split(wide):
        return [wide[:, C * j : C * j + C] for j in range(wide.shape[1] // C)]

    def rim(above, below):
        return split(jnp.where(iota(above.shape, 0) >= 4, above, below))

    def unpack(packed, high, count=4):
        packed = packed.astype(F32)
        pieces = []
        for i in range(count):
            piece = packed[i // 2 * 8 : i // 2 * 8 + 8]
            pieces.append(pltpu.roll(piece, 4, 0) if (i % 2 == 1) != high else piece)
        return jnp.concatenate(pieces, axis=1)

    def labels_of(above, own):
        above, own = above[...].astype(F32).T, own[...].astype(F32).T
        rows = jnp.concatenate([above[56:64], own], axis=0)
        rows = pltpu.roll(rows.reshape(9, 8, 16), 4, 1).reshape(72, 16)
        spot = iota((72, 1), 0)
        at_end = ((spot < 8) & (row == 0)) | ((spot >= 64) & (row == nrow - 1))
        return rows * 4.0 + jnp.where((spot % 8 < 4) & at_end, 2.0, 0.0)

    def attend(spans, real, nx, column_of, base, table_of, marks, blocks):
        nq = nx * 8
        per = 128 // nq
        wide = -(-HEADS // per)
        heads = [list(range(m * per, min(HEADS, m * per + per))) for m in range(wide)]
        count = len(spans)
        lanes = iota((72, 256), 1)
        pieces = []
        for x in range(WIN):
            value = ext[column_of(x)]
            turned = jnp.concatenate([value[64:72], value[0:64]], axis=0)
            value = jnp.where(iota((72, 256), 0) % 8 < 4, value, turned)
            mark = ((lanes - C).astype(F32) == marks[:, x : x + 1]).astype(F32)
            pieces.append(jnp.where(lanes >= C, mark, value))
        tokens = jnp.concatenate(
            [pieces[x][8 * a : 8 * a + 8] for a in spans[:real] for x in range(WIN)], axis=0
        ).astype(BF16)
        asking = jnp.concatenate(
            [pieces[x][8 * a : 8 * a + 8] for a in spans for x in range(nx)], axis=0
        ).astype(BF16)
        keys = dot(tokens, wk[...]).astype(BF16)
        queries = lax.dot_general(wq[...], asking, NT, preferred_element_type=F32)
        values = lax.dot_general(wv[...], tokens, NT, preferred_element_type=F32)

        block = iota((16, 128), 1) // nq
        block32 = iota((HD, 128), 1) // nq
        for g in range(count // per):
            some = queries[:, 128 * g : 128 * g + 128]
            turns = [some] + [pltpu.roll(some, k * nq, 1) for k in range(1, per)]
            for s in range(min(per, real - per * g)):
                w = per * g + s
                code = turns[(0 - s) % per][C:]
                for t in range(1, per):
                    code = jnp.where(block == t, turns[(t - s) % per][C:], code)
                code = code.astype(BF16)
                for m in range(wide):
                    part = [
                        jnp.where(block32 == h % per, turns[(h - s) % per][h * HD : h * HD + HD], 0.0)
                        for h in heads[m]
                    ]
                    low = heads[m][0] * HD
                    blocks[w, low : low + HD * len(part), 128 * m : 128 * m + 128] = jnp.concatenate(
                        part, axis=0
                    ).astype(BF16)
                    blocks[w, C : C + 16, 128 * m : 128 * m + 128] = code
        table = table_of()
        for w in range(real):
            scores = dot(keys[w * 64 : w * 64 + 64], blocks[w])
            scores_v[w, :, 0 : 128 * wide] = scores * (HD ** (-0.5) * LOG2E) + table
        powers = []
        for w in range(real):
            scores = scores_v[w, :, 0 : 128 * wide]
            powers.append(jnp.exp2(scores - jnp.max(scores, axis=0, keepdims=True)).astype(BF16))
        one = jnp.ones((16, 64), BF16)
        found = []
        for w in range(real):
            mine = values[:, w * 64 : w * 64 + 64].astype(BF16)
            for m in range(wide):
                low, high = heads[m][0] * HD, heads[m][-1] * HD + HD
                sums = dot(jnp.concatenate([mine[low:high], one], axis=0), powers[w][:, 128 * m : 128 * m + 128])
                found.append(sums[0 : high - low] * (1.0 / sums[high - low : high - low + 1]))
        turned = []
        for g in range(count // per):
            rows_of = []
            for h in range(HEADS):
                m, i = h // per, h % per
                row_block = None
                for s in range(min(per, real - per * g)):
                    piece = found[(per * g + s) * wide + m][i * HD : i * HD + HD]
                    if (s - h) % per:
                        piece = pltpu.roll(piece, ((s - h) % per) * nq, 1)
                    row_block = piece if s == 0 else jnp.where(block32 == s, piece, row_block)
                rows_of.append(row_block)
            turned.append(jnp.concatenate(rows_of, axis=0))
        attended = jnp.concatenate(turned, axis=1).astype(BF16).T
        mixed = dot(attended, proj_v[...])
        for w, a in enumerate(spans[:real]):
            for x in range(nx):
                spot = w * nq + x * 8
                branch[base + x, 8 * a : 8 * a + 8] = mixed[spot : spot + 8]

    def finish(f, size):
        lanes = pl.ds(f * 768 if isinstance(f, int) else pl.multiple_of(f * 768, 768), size * C)
        columns = split(tok_v[:, lanes].astype(F32))
        upper = iota((64, C), 0) % 8 < 4
        residual = jnp.concatenate(
            [
                columns[j] + jnp.where(upper, branch[4 * f + j, 0:64], branch[4 * f + j, 8:72])
                for j in range(size)
            ],
            axis=0,
        )
        high = residual.astype(BF16)
        low = (residual - high.astype(F32)).astype(BF16)
        centred = residual - (mean(high) + mean(low))
        variance = mean((centred * centred).astype(BF16))
        second = (centred * lax.rsqrt(variance + 1e-05) * g2_v[...].reshape(1, C)).astype(BF16)
        done = residual
        for n in range(0, HID, 256):
            hidden = in_pieces(32, gelu, dot(second, up_v[:, n : n + 256]))
            done = done + lax.dot_general(hidden, down_v[:, n : n + 256], NT, preferred_element_type=F32)
        out[:, lanes] = jnp.concatenate([done[j * 64 : j * 64 + 64] for j in range(size)], axis=1).astype(BF16)

    place(split(tok_v[...].astype(F32)), 4, 0)

    @pl.when(jnp.logical_not(early))
    def _():
        pl.semaphore_wait(barrier, expected)
        pl.when(col == ncol - 2)(functools.partial(meet, 0))
        send_but_first(ROWS)
        send(EAST)
        pl.when(jnp.logical_not(oldest))(functools.partial(send_but_first, WEST))

    loads[7].wait()
    attend([1, 2, 3, 4, 5, 6, 7, 7], 7, 8, lambda x: 8 + x, 4, lambda: bias[...], labels_of(lab_v, lab_v), blocks64)

    @pl.when(newest)
    def _():
        pl.semaphore_wait(met_sem, 1)
        send(ROWS)
        send(WEST)

    @pl.when(near_first)
    def _():
        pl.semaphore_wait(first_sem, 1)
        pl.when(oldest)(functools.partial(send_first, ROWS))
        pl.when(jnp.logical_not(oldest))(functools.partial(send_first, WEST))

    arrive(ROWS)
    marks = labels_of(tlab, lab_v)
    place_x = iota((72, 8), 1)
    groups[1] = marks[:, 8:16] + jnp.where((place_x >= 4) & newest, 1.0, 0.0)
    place(rim(unpack(top[...], True), unpack(bot[...], False)), 4, 64)
    attend([0, 8], 2, 8, lambda x: 8 + x, 4, lambda: bias[...], marks, blocks64)
    for load in loads[8:]:
        load.wait()
    finish(1, 8)

    def edge(i, carry):
        side = jnp.where(oldest, 1 - i, i)

        @pl.when(side == 1)
        def _():
            arrive(WEST)

        @pl.when((side == 0) & oldest)
        def _():
            pl.semaphore_wait(met_sem, 3)
            send(WEST)

        @pl.when(side == 0)
        def _():
            arrive(EAST[2:4])
            near = labels_of(ltlab, llab)
            near = jnp.concatenate([near[:, 12:16], near[:, 8:12]], axis=1)
            groups[0] = near + jnp.where((place_x < 4) & oldest, 1.0, 0.0)
            arrive(EAST[0:2])
            arrive(EAST[4:5])

        edges = rim(unpack(corner[side, 0], True, 3), unpack(corner[side, 1], False, 3))
        near = split(beside[side].astype(F32))
        place([jnp.concatenate(pair, axis=0) for pair in zip(near, edges)], 20 * side, 0)
        attend(
            list(range(9)) + [8] * 3, 9, 4,
            lambda x: 16 * side + x + (1 - side) * (4 if x < 4 else -4),
            12 * side, lambda: bias_s[side], groups[side], blocks32,
        )
        finish(3 * side, 4)
        return carry

    lax.fori_loop(0, 2, edge, 0)
    for copy in copies:
        copy.wait_send()


def local(nrow, ncol, tok, lab, gain_one, qkv, proj, table, gain_two, up, down):
    args = (tok, lab.T, gain_one, qkv, proj, table, gain_two, up, down.T)
    vmem = pltpu.VMEM
    scratch = [vmem(a.shape, a.dtype) for a in args]
    args = [pltpu.with_memory_space_constraint(a, pltpu.HBM) for a in args]
    scratch += [vmem((2, 64, 768), BF16), vmem((2, 2, 16, 256), BF16)] + [vmem((16, 768), BF16)] * 2
    scratch += [vmem((16, 64), jnp.int32)] * 3
    scratch += [vmem((16, 768), BF16)] * 2 + [vmem((16, 256), BF16)] * 4
    scratch += [vmem((24, 72, 256), F32), vmem((16, 72, C), F32), vmem((2, 72, 8), F32)]
    scratch += [vmem((C + 16, 256), BF16), vmem((C, 256), BF16), vmem((256, 256), BF16)]
    scratch += [vmem((8, 8, 128), F32), vmem((64, 384), F32), vmem((2, 64, 256), F32)]
    scratch += [vmem((10, 256, 384), BF16), vmem((12, 256, 256), BF16), vmem((12, 64, 384), F32)]
    scratch += [pltpu.SemaphoreType.DMA((13,)), pltpu.SemaphoreType.DMA((11,)), pltpu.SemaphoreType.DMA((11,))]
    scratch += [pltpu.SemaphoreType.REGULAR] * 2
    return pl.pallas_call(
        functools.partial(kernel, nrow, ncol),
        out_shape=vmem((64, 3072), BF16),
        in_specs=[pl.BlockSpec(memory_space=pltpu.HBM)] * len(args),
        out_specs=pl.BlockSpec(memory_space=vmem),
        scratch_shapes=scratch,
        compiler_params=pltpu.CompilerParams(
            collective_id=0, has_side_effects=True, vmem_limit_bytes=56 * 1024 * 1024
        ),
        name="window_block",
    )(*args)


def solution(mesh):
    placed = (P("row", "col"), P("row", "col"), P(), P(), P(), P(), P(), P(), P())
    return jax.shard_map(
        functools.partial(local, mesh.shape["row"], mesh.shape["col"]),
        mesh=mesh, in_specs=placed, out_specs=P("row", "col"), check_vma=False,
    )
```

```python
import functools

import jax
import jax.numpy as jnp
from jax import lax
from jax.experimental import pallas as pl
from jax.experimental.pallas import tpu as pltpu
from jax.sharding import PartitionSpec as P

C = 192
HEADS = 6
HID = 768
WIN = 8
HD = 32
MESH = pl.DeviceIdType.MESH
F32 = jnp.float32
BF16 = jnp.bfloat16
LOG2E = 1.4426950408889634
FAR = -1e30
NT = (((1,), (1,)), ((), ()))
LOGIT = (
    -2.3022072315216064, -0.10483857989311218, 9.559292084304616e-05, 0.00015938941214699298,
    -1.1452430044300854e-05, 3.8504501276293013e-07, -5.209909392789314e-09,
)


def iota(shape, axis):
    return lax.broadcasted_iota(jnp.int32, shape, axis)


def dot(a, b):
    return jnp.dot(a, b, preferred_element_type=F32)


def in_pieces(step, apply, *arrays):
    return jnp.concatenate(
        [apply(*(a[i : i + step] for a in arrays)) for i in range(0, arrays[0].shape[0], step)], axis=0
    )


def gelu(v):
    square = v * v
    logit = LOGIT[6] * square + LOGIT[5]
    for k in range(4, -1, -1):
        logit = logit * square + LOGIT[k]
    return (v * (1.0 / (1.0 + jnp.exp2(v * logit)))).astype(BF16)


def kernel(
    nrow, ncol,
    tok, lab, gain_one, qkv, proj, table, gain_two, up, down,
    out,
    tok_v, lab_v, g1_v, qkv_v, proj_v, tab_v, g2_v, up_v, down_v,
    beside, corner, top, bot, llab, tlab, ltlab,
    last_all, first_all, last_east, first_east, last_west, first_west,
    ext, branch, groups, wq, wv, wk, gath, bias, bias_s, blocks64, blocks32, scores_v,
    in_sem, send_sem, recv_sem, met_sem, first_sem, down_t,
):
    row, col = lax.axis_index("row"), lax.axis_index("col")
    newest, oldest = col == ncol - 1, col == 0
    corner_row = (row <= 1) | (row == nrow - 1)
    first = (row == 0) & oldest
    near_first = corner_row & (col <= 1) & jnp.logical_not(first)
    early = newest | first

    def at(dr, dc):
        return (lax.rem(row + dr + nrow, nrow), lax.rem(col + dc + ncol, ncol))

    barrier = pltpu.get_barrier_semaphore()

    def greet(dr, dc):
        pl.semaphore_signal(barrier, inc=1, device_id=at(dr, dc), device_id_type=MESH)

    for dr in (0, 1, -1):
        greet(dr, -1)
    expected = jnp.where(newest, 3, jnp.where(oldest, 5, 8)) - near_first.astype(jnp.int32)
    foot, crown, waist = pl.ds(48, 16), pl.ds(0, 16), pl.ds(16, 32)
    whole = pl.ds(0, 64)
    west, east = pl.ds(0, 4 * C), pl.ds(12 * C, 4 * C)
    moves = [
        (last_east, corner.at[0, 0], (1, 1)),
        (first_east, corner.at[0, 1], (-1, 1)),
        (lab, ltlab, (1, 1)),
        (lab, llab, (0, 1)),
        (tok.at[whole, east], beside.at[0], (0, 1)),
        (last_all, top, (1, 0)),
        (first_all, bot, (-1, 0)),
        (lab, tlab, (1, 0)),
        (last_west, corner.at[1, 0], (1, -1)),
        (first_west, corner.at[1, 1], (-1, -1)),
        (tok.at[whole, west], beside.at[1], (0, -1)),
    ]
    copies = [
        pltpu.make_async_remote_copy(
            src_ref=src, dst_ref=dst, send_sem=send_sem.at[i], recv_sem=recv_sem.at[i],
            device_id=at(*where), device_id_type=MESH,
        )
        for i, (src, dst, where) in enumerate(moves)
    ]
    EAST, ROWS, WEST = range(0, 5), range(5, 8), range(8, 11)

    def send(group):
        for i in group:
            copies[i].start()

    def send_but_first(group):
        for i in group:
            dr, dc = moves[i][2]
            to = at(dr, dc)
            pl.when((to[0] != 0) | (to[1] != 0))(copies[i].start)

    def send_first(group):
        for i in group:
            dr, dc = moves[i][2]
            to = at(dr, dc)
            pl.when((to[0] == 0) & (to[1] == 0))(copies[i].start)

    def arrive(group):
        for i in group:
            copies[i].wait_recv()

    def meet(dr):
        pl.semaphore_signal(met_sem, inc=1, device_id=at(dr, 1), device_id_type=MESH)

    def pack(rows, high, width, packed):
        rows = rows.astype(F32)
        turned = pltpu.roll(rows, 4, 0)
        low, high = (turned, rows) if high else (rows, turned)
        pieces = []
        for i in range(0, rows.shape[1], 2 * width):
            below = high[:, i + width : i + 2 * width]
            if below.shape[1] == 0:
                below = high[:, i : i + width]
            pieces.append(jnp.where(iota((8, width), 0) < 4, low[:, i : i + width], below))
        packed[...] = jnp.concatenate(pieces, axis=0).astype(BF16)

    edges = [
        pltpu.make_async_copy(tok.at[rows, east], tok_v.at[rows, east], in_sem.at[11 + i])
        for i, rows in enumerate((foot, crown))
    ]

    @pl.when(early)
    def _():
        pl.semaphore_wait(barrier, expected)
        for edge in edges:
            edge.start()
        for edge in edges:
            edge.wait()
        pack(tok_v[48:64, 12 * C :][8:16], True, 256, last_east)
        pack(tok_v[0:16, 12 * C :][0:8], False, 256, first_east)
        send(EAST)

        @pl.when(newest)
        def _():
            for dr in (0, 1, -1):
                meet(dr)

        @pl.when(first)
        def _():
            for dr, dc in ((1, 0), (-1, 0), (0, 1), (1, 1), (-1, 1)):
                pl.semaphore_signal(first_sem, inc=1, device_id=at(dr, dc), device_id_type=MESH)

    for dr in (0, 1, -1):
        pl.when(jnp.logical_not(newest | (col == ncol - 2) | first))(functools.partial(greet, dr, 1))
        if dr:
            pl.when(jnp.logical_not(newest | first))(functools.partial(greet, dr, 0))
    loads = [
        pltpu.make_async_copy(src, dst, in_sem.at[i])
        for i, (src, dst) in enumerate([
            (tok.at[foot], tok_v.at[foot]), (tok.at[crown], tok_v.at[crown]), (tok.at[waist], tok_v.at[waist]),
            (lab, lab_v), (table, tab_v), (qkv, qkv_v), (gain_one, g1_v),
            (proj, proj_v), (gain_two, g2_v), (up, up_v), (down, down_v),
        ])
    ]
    for load in loads:
        load.start()

    loads[0].wait()
    loads[1].wait()

    pack(tok_v[48:64][8:16], True, 768, last_all)
    pack(tok_v[0:16][0:8], False, 768, first_all)
    pack(tok_v[48:64, 0 : 4 * C][8:16], True, 256, last_west)
    pack(tok_v[0:16, 0 : 4 * C][0:8], False, 256, first_west)

    @pl.when(jnp.logical_not(early))
    def _():
        pack(tok_v[48:64, 12 * C :][8:16], True, 256, last_east)
        pack(tok_v[0:16, 12 * C :][0:8], False, 256, first_east)

    pl.when(first)(functools.partial(send, ROWS))
    for load in loads[2:7]:
        load.wait()

    eye = (iota((16, 64), 0) == iota((16, 64), 1)).astype(F32)
    apart = jnp.where(iota((64, 64), 0) < 16, (iota((64, 64), 0) != iota((64, 64), 1)).astype(F32) * FAR, 0.0)
    weights = qkv_v[...].astype(F32)
    pad = jnp.zeros((C, 64), F32)
    wq[0:C] = jnp.concatenate([weights[:, 0:C].T, pad], axis=1).astype(BF16)
    wq[C : C + 16] = jnp.concatenate([jnp.zeros((16, C), F32), eye], axis=1).astype(BF16)
    wv[...] = jnp.concatenate([weights[:, 2 * C : 3 * C].T, pad], axis=1).astype(BF16)
    wk[0:C] = jnp.concatenate([weights[:, C : 2 * C], pad], axis=1).astype(BF16)
    wk[C : C + 64] = jnp.concatenate([jnp.zeros((64, C), F32), apart], axis=1).astype(BF16)
    blocks64[...] = jnp.zeros(blocks64.shape, BF16)
    blocks32[...] = jnp.zeros(blocks32.shape, BF16)

    spread = jnp.concatenate([tab_v[...] * LOG2E, jnp.zeros((HEADS, 256 - 225), F32)], axis=1)
    spread = jnp.concatenate([spread, jnp.zeros((8 - HEADS, 256), F32)], axis=0)
    rows = jnp.concatenate([pltpu.roll(spread, 15 * ((s + 4) % 8), 1) if s != 4 else spread for s in range(WIN)], axis=0)
    lane = iota((256, 128), 1)
    select = (iota((256, 128), 0) == ((lane % 8 + 4) % 8 + 7) * 15 + lane // 8).astype(F32)
    gath[...] = jnp.dot(rows, select, precision=lax.Precision.HIGHEST).reshape(8, 8, 128)
    bias_s[...] = jnp.zeros(bias_s.shape, F32)
    for h in range(HEADS):
        strip = gath[:, h, :]
        for x in range(WIN):
            part = strip[:, (7 - x) * 8 : (7 - x) * 8 + 64]
            other = (x + 4) % 8
            bias[x * 8 : x * 8 + 8, h * 64 : h * 64 + 64] = part
            bias_s[1, x * 8 : x * 8 + 8, h * 32 : h * 32 + 32] = part[:, 0:32]
            bias_s[0, other * 8 : other * 8 + 8, h * 32 : h * 32 + 32] = part[:, 32:64]

    gain = g1_v[...].reshape(1, C)
    unit = jnp.ones((C, 128), BF16)

    def mean(values):
        total = dot(values, unit) * (1.0 / C)
        return jnp.concatenate([total, total[:, 0 : C - 128]], axis=1)

    def place(columns, base, start):
        size = columns[0].shape[0]
        tokens = jnp.concatenate(columns, axis=0)
        centred = tokens - mean(tokens.astype(BF16))
        normed = centred * lax.rsqrt(mean((centred * centred).astype(BF16)) + 1e-05) * gain
        for j in range(len(columns)):
            ext[base + j, start : start + size, 0:C] = normed[j * size : j * size + size]

    def split(wide):
        return [wide[:, C * j : C * j + C] for j in range(wide.shape[1] // C)]

    def rim(above, below):
        return split(jnp.where(iota(above.shape, 0) >= 4, above, below))

    def unpack(packed, high, count=4):
        packed = packed.astype(F32)
        pieces = []
        for i in range(count):
            piece = packed[i // 2 * 8 : i // 2 * 8 + 8]
            pieces.append(pltpu.roll(piece, 4, 0) if (i % 2 == 1) != high else piece)
        return jnp.concatenate(pieces, axis=1)

    def labels_of(above, own):
        above, own = above[...].astype(F32).T, own[...].astype(F32).T
        rows = jnp.concatenate([above[56:64], own], axis=0)
        rows = pltpu.roll(rows.reshape(9, 8, 16), 4, 1).reshape(72, 16)
        spot = iota((72, 1), 0)
        at_end = ((spot < 8) & (row == 0)) | ((spot >= 64) & (row == nrow - 1))
        return rows * 4.0 + jnp.where((spot % 8 < 4) & at_end, 2.0, 0.0)

    def attend(spans, real, nx, column_of, base, table_of, marks, blocks):
        nq = nx * 8
        per = 128 // nq
        wide = -(-HEADS // per)
        heads = [list(range(m * per, min(HEADS, m * per + per))) for m in range(wide)]
        count = len(spans)
        lanes = iota((72, 256), 1)
        pieces = []
        for x in range(WIN):
            value = ext[column_of(x)]
            turned = jnp.concatenate([value[64:72], value[0:64]], axis=0)
            value = jnp.where(iota((72, 256), 0) % 8 < 4, value, turned)
            mark = ((lanes - C).astype(F32) == marks[:, x : x + 1]).astype(F32)
            pieces.append(jnp.where(lanes >= C, mark, value))
        tokens = jnp.concatenate(
            [pieces[x][8 * a : 8 * a + 8] for a in spans[:real] for x in range(WIN)], axis=0
        ).astype(BF16)
        asking = jnp.concatenate(
            [pieces[x][8 * a : 8 * a + 8] for a in spans for x in range(nx)], axis=0
        ).astype(BF16)
        keys = dot(tokens, wk[...]).astype(BF16)
        queries = lax.dot_general(wq[...], asking, NT, preferred_element_type=F32)
        values = lax.dot_general(wv[...], tokens, NT, preferred_element_type=F32)

        block = iota((16, 128), 1) // nq
        block32 = iota((HD, 128), 1) // nq
        for g in range(count // per):
            some = queries[:, 128 * g : 128 * g + 128]
            turns = [some] + [pltpu.roll(some, k * nq, 1) for k in range(1, per)]
            for s in range(min(per, real - per * g)):
                w = per * g + s
                code = turns[(0 - s) % per][C:]
                for t in range(1, per):
                    code = jnp.where(block == t, turns[(t - s) % per][C:], code)
                code = code.astype(BF16)
                for m in range(wide):
                    part = [
                        jnp.where(block32 == h % per, turns[(h - s) % per][h * HD : h * HD + HD], 0.0)
                        for h in heads[m]
                    ]
                    low = heads[m][0] * HD
                    blocks[w, low : low + HD * len(part), 128 * m : 128 * m + 128] = jnp.concatenate(
                        part, axis=0
                    ).astype(BF16)
                    blocks[w, C : C + 16, 128 * m : 128 * m + 128] = code
        table = table_of()
        for w in range(real):
            scores = dot(keys[w * 64 : w * 64 + 64], blocks[w])
            scores_v[w, :, 0 : 128 * wide] = scores * (HD ** (-0.5) * LOG2E) + table
        powers = []
        for w in range(real):
            scores = scores_v[w, :, 0 : 128 * wide]
            powers.append(jnp.exp2(scores - jnp.max(scores, axis=0, keepdims=True)).astype(BF16))
        one = jnp.ones((16, 64), BF16)
        found = []
        for w in range(real):
            mine = values[:, w * 64 : w * 64 + 64].astype(BF16)
            for m in range(wide):
                low, high = heads[m][0] * HD, heads[m][-1] * HD + HD
                sums = dot(jnp.concatenate([mine[low:high], one], axis=0), powers[w][:, 128 * m : 128 * m + 128])
                found.append(sums[0 : high - low] * (1.0 / sums[high - low : high - low + 1]))
        turned = []
        for g in range(count // per):
            rows_of = []
            for h in range(HEADS):
                m, i = h // per, h % per
                row_block = None
                for s in range(min(per, real - per * g)):
                    piece = found[(per * g + s) * wide + m][i * HD : i * HD + HD]
                    if (s - h) % per:
                        piece = pltpu.roll(piece, ((s - h) % per) * nq, 1)
                    row_block = piece if s == 0 else jnp.where(block32 == s, piece, row_block)
                rows_of.append(row_block)
            turned.append(jnp.concatenate(rows_of, axis=0))
        attended = jnp.concatenate(turned, axis=1).astype(BF16).T
        mixed = dot(attended, proj_v[...])
        for w, a in enumerate(spans[:real]):
            for x in range(nx):
                spot = w * nq + x * 8
                branch[base + x, 8 * a : 8 * a + 8] = mixed[spot : spot + 8]

    def finish(f, size):
        lanes = pl.ds(f * 768 if isinstance(f, int) else pl.multiple_of(f * 768, 768), size * C)
        columns = split(tok_v[:, lanes].astype(F32))
        upper = iota((64, C), 0) % 8 < 4
        residual = jnp.concatenate(
            [
                columns[j] + jnp.where(upper, branch[4 * f + j, 0:64], branch[4 * f + j, 8:72])
                for j in range(size)
            ],
            axis=0,
        )
        high = residual.astype(BF16)
        low = (residual - high.astype(F32)).astype(BF16)
        centred = residual - (mean(high) + mean(low))
        variance = mean((centred * centred).astype(BF16))
        second = (centred * lax.rsqrt(variance + 1e-05) * g2_v[...].reshape(1, C)).astype(BF16)
        done = residual
        for n in range(0, HID, 256):
            hidden = in_pieces(32, gelu, dot(second, up_v[:, n : n + 256]))
            done = done + dot(hidden, down_t[n : n + 256])
        out[:, lanes] = jnp.concatenate([done[j * 64 : j * 64 + 64] for j in range(size)], axis=1).astype(BF16)

    place(split(tok_v[...].astype(F32)), 4, 0)

    @pl.when(jnp.logical_not(early))
    def _():
        pl.semaphore_wait(barrier, expected)
        pl.when(col == ncol - 2)(functools.partial(meet, 0))
        send_but_first(ROWS)
        send(EAST)
        pl.when(jnp.logical_not(oldest))(functools.partial(send_but_first, WEST))

    loads[7].wait()
    attend([1, 2, 3, 4, 5, 6, 7, 7], 7, 8, lambda x: 8 + x, 4, lambda: bias[...], labels_of(lab_v, lab_v), blocks64)

    @pl.when(newest)
    def _():
        pl.semaphore_wait(met_sem, 1)
        send(ROWS)
        send(WEST)

    @pl.when(near_first)
    def _():
        pl.semaphore_wait(first_sem, 1)
        pl.when(oldest)(functools.partial(send_first, ROWS))
        pl.when(jnp.logical_not(oldest))(functools.partial(send_first, WEST))

    arrive(ROWS)
    marks = labels_of(tlab, lab_v)
    place_x = iota((72, 8), 1)
    groups[1] = marks[:, 8:16] + jnp.where((place_x >= 4) & newest, 1.0, 0.0)
    place(rim(unpack(top[...], True), unpack(bot[...], False)), 4, 64)
    attend([0, 8], 2, 8, lambda x: 8 + x, 4, lambda: bias[...], marks, blocks64)
    for load in loads[8:]:
        load.wait()
    down_t[...] = down_v[...].T
    finish(1, 8)

    def edge(i, carry):
        side = jnp.where(oldest, 1 - i, i)

        @pl.when(side == 1)
        def _():
            arrive(WEST)

        @pl.when((side == 0) & oldest)
        def _():
            pl.semaphore_wait(met_sem, 3)
            send(WEST)

        @pl.when(side == 0)
        def _():
            arrive(EAST[2:4])
            near = labels_of(ltlab, llab)
            near = jnp.concatenate([near[:, 12:16], near[:, 8:12]], axis=1)
            groups[0] = near + jnp.where((place_x < 4) & oldest, 1.0, 0.0)
            arrive(EAST[0:2])
            arrive(EAST[4:5])

        edges = rim(unpack(corner[side, 0], True, 3), unpack(corner[side, 1], False, 3))
        near = split(beside[side].astype(F32))
        place([jnp.concatenate(pair, axis=0) for pair in zip(near, edges)], 20 * side, 0)
        attend(
            list(range(9)) + [8] * 3, 9, 4,
            lambda x: 16 * side + x + (1 - side) * (4 if x < 4 else -4),
            12 * side, lambda: bias_s[side], groups[side], blocks32,
        )
        finish(3 * side, 4)
        return carry

    lax.fori_loop(0, 2, edge, 0)
    for copy in copies:
        copy.wait_send()


def local(nrow, ncol, tok, lab, gain_one, qkv, proj, table, gain_two, up, down):
    args = (tok, lab.T, gain_one, qkv, proj, table, gain_two, up, down.T)
    vmem = pltpu.VMEM
    scratch = [vmem(a.shape, a.dtype) for a in args]
    args = [pltpu.with_memory_space_constraint(a, pltpu.HBM) for a in args]
    scratch += [vmem((2, 64, 768), BF16), vmem((2, 2, 16, 256), BF16)] + [vmem((16, 768), BF16)] * 2
    scratch += [vmem((16, 64), jnp.int32)] * 3
    scratch += [vmem((16, 768), BF16)] * 2 + [vmem((16, 256), BF16)] * 4
    scratch += [vmem((24, 72, 256), F32), vmem((16, 72, C), F32), vmem((2, 72, 8), F32)]
    scratch += [vmem((C + 16, 256), BF16), vmem((C, 256), BF16), vmem((256, 256), BF16)]
    scratch += [vmem((8, 8, 128), F32), vmem((64, 384), F32), vmem((2, 64, 256), F32)]
    scratch += [vmem((10, 256, 384), BF16), vmem((12, 256, 256), BF16), vmem((12, 64, 384), F32)]
    scratch += [pltpu.SemaphoreType.DMA((13,)), pltpu.SemaphoreType.DMA((11,)), pltpu.SemaphoreType.DMA((11,))]
    scratch += [pltpu.SemaphoreType.REGULAR] * 2 + [vmem((HID, C), BF16)]
    return pl.pallas_call(
        functools.partial(kernel, nrow, ncol),
        out_shape=vmem((64, 3072), BF16),
        in_specs=[pl.BlockSpec(memory_space=pltpu.HBM)] * len(args),
        out_specs=pl.BlockSpec(memory_space=vmem),
        scratch_shapes=scratch,
        compiler_params=pltpu.CompilerParams(
            collective_id=0, has_side_effects=True, vmem_limit_bytes=56 * 1024 * 1024
        ),
        name="window_block",
    )(*args)


def solution(mesh):
    placed = (P("row", "col"), P("row", "col"), P(), P(), P(), P(), P(), P(), P())
    return jax.shard_map(
        functools.partial(local, mesh.shape["row"], mesh.shape["col"]),
        mesh=mesh, in_specs=placed, out_specs=P("row", "col"), check_vma=False,
    )
```
